128 devices in a mesh: dp: 32 (over y, z, x_hi), tensor: 4 (over x_lo, core).
Axes of the slice: x: 4 (x_hi: 2, x_lo: 2; x = x_hi * 2 + x_lo), y: 4, z: 4, core: 2. Of those that a mesh axis runs over, the one named last changes fastest.
Arguments:
- inputs: float32 [50176, 1024], P('dp'), may hold values from -6 to 6
- w_qkv: bfloat16 [1024, 3, 1024], P('dp', None, 'tensor'), may hold values from -0.1875 to 0.1875
- w_out: bfloat16 [1024, 1024], P('dp', 'tensor'), may hold values from -0.75 to 0.75
- w_fc1: bfloat16 [1024, 4096], P('dp', 'tensor'), may hold values from -0.1875 to 0.1875
- w_fc2: bfloat16 [1024, 4096], P('dp', 'tensor'), may hold values from -0.09375 to 0.09375
- w_map: bfloat16 [1024, 8], P('dp', 'tensor'), may hold values from -0.1875 to 0.1875
- norm_gains: float32 [3, 1024], replicated, may hold values from 0.25 to 1.75
- norm_biases: float32 [3, 1024], replicated, may hold values from -3 to 3
- keep_mask: int32 [256, 196], P('dp'), may hold values from 0 to 1, as said below
- d_tokens: float32 [256, 8, 1024], P('dp', 'tensor'), may hold values from -6 to 6
Outputs:
- learned: float32 [256, 8, 1024], P('dp', 'tensor')
- d_inputs: float32 [50176, 1024], P('dp')
- d_qkv: float32 [1024, 3, 1024], P('dp', None, 'tensor')
- d_out: float32 [1024, 1024], P('dp', 'tensor')
- d_fc1: float32 [1024, 4096], P('dp', 'tensor')
- d_fc2: float32 [1024, 4096], P('dp', 'tensor')
- d_map: float32 [1024, 8], P('dp', 'tensor')
- d_gains: float32 [3, 1024], replicated
- d_biases: float32 [3, 1024], replicated
The draws below stay inside these ranges and needn't reach their ends.
Inputs may be any that keep to these rules, and one draw needn't show every extreme that they name: `keep_mask`: 1 keeps a patch and 0 drops it; every image drops between 19 and 78 of its patches, and some image drops each of these two numbers.
All inputs are finite; a program needn't handle non-finite values.
Results may differ from the reference program's by a relative error of at most 0.014.
Values may be sent and summed in bfloat16 or wider, within the bound.
A program may use at most 192 MiB of HBM per device.

```python
import jax
import jax.numpy as jnp
from jax import lax

D = 1024
HEADS = 16
HEAD_DIM = 64
MLP = 4096
MAPS = 8
PATCHES = 196
IMAGES = 256
TOKENS = 50176


def draw_keep_mask(key, part):
    key = jax.random.fold_in(key, 11)
    key_count, key_order, key_patch = jax.random.split(key, 3)
    least_drop = PATCHES // 10
    most_drop = 2 * PATCHES // 5
    drop_counts = jax.random.randint(key_count, (IMAGES,), least_drop, most_drop + 1)
    image_scores = jax.random.randint(key_order, (IMAGES,), 0, 1 << 20) * IMAGES + jnp.arange(IMAGES)
    image_order = jnp.argsort(image_scores, stable=True)
    drop_counts = drop_counts.at[image_order[0]].set(least_drop).at[image_order[1]].set(most_drop)
    patch_scores = jax.random.randint(key_patch, (IMAGES, PATCHES), 0, 1 << 20) * PATCHES + jnp.arange(PATCHES)[None, :]
    patch_ranks = jnp.argsort(jnp.argsort(patch_scores, axis=1, stable=True), axis=1, stable=True)
    return (patch_ranks >= drop_counts[:, None]).astype(jnp.int32)


def block_scale(stream_key, extent, pieces, least, largest):
    factor_of, own = 1.0, jax.random.fold_in(stream_key, 6)
    for position, parts in pieces:
        steps = jnp.exp(jax.random.uniform(jax.random.fold_in(own, position), (parts,), jnp.float32, least / len(pieces), largest / len(pieces)))
        factor_of = factor_of * jnp.repeat(steps, extent[position] // parts).reshape([-1 if axis == position else 1 for axis in range(len(extent))])
    return factor_of


def gaussian(rng, extent, spread, reach, pieces=(), kind=jnp.bfloat16):
    level = block_scale(rng, extent, pieces, -0.22, 0.18) if pieces else 1.0
    entries = jax.random.normal(rng, extent, jnp.float32) * spread * level
    return jnp.minimum(jnp.maximum(entries, -reach), reach).astype(kind)


def setup_inputs(seed: int = 0) -> dict:
    streams_of = jax.random.split(jax.random.key(seed), 11)
    inputs = gaussian(streams_of[0], (TOKENS, D), 1.0, 6.0, ((0, 32),), jnp.float32)
    w_qkv = gaussian(streams_of[1], (D, 3, D), D ** -0.5, 0.1875, ((0, 32), (2, 4)))
    w_out = gaussian(streams_of[2], (D, D), (D // 16) ** -0.5, 0.75, ((0, 32), (1, 4)))
    w_fc1 = gaussian(streams_of[3], (D, MLP), D ** -0.5, 0.1875, ((0, 32), (1, 4)))
    w_fc2 = gaussian(streams_of[4], (D, MLP), MLP ** -0.5, 0.09375, ((0, 32), (1, 4)))
    w_map = gaussian(streams_of[5], (D, MAPS), D ** -0.5, 0.1875, ((0, 32), (1, 4)))
    norm_gains = jnp.clip(1.0 + 0.15 * jax.random.normal(streams_of[6], (3, D), jnp.float32), 0.25, 1.75)
    norm_biases = gaussian(streams_of[7], (3, D), 0.5, 3.0, (), jnp.float32)
    keep_mask = draw_keep_mask(jax.random.fold_in(streams_of[10], 71), 0)
    d_tokens = gaussian(streams_of[9], (IMAGES, MAPS, D), 1.0, 6.0, ((0, 32), (1, 4)), jnp.float32)
    return dict(inputs=inputs, w_qkv=w_qkv, w_out=w_out, w_fc1=w_fc1, w_fc2=w_fc2, w_map=w_map, norm_gains=norm_gains, norm_biases=norm_biases, keep_mask=keep_mask, d_tokens=d_tokens)


@jax.custom_vjp
def low(v):
    return lax.optimization_barrier(v.astype(jnp.bfloat16)).astype(jnp.float32)

@jax.custom_vjp
def low_back(v):
    return v

def low_keep(v):
    return (low(v), None)

def low_pass(kept, grad):
    return (grad,)

def back_keep(v):
    return (v, None)

def back_low(kept, grad):
    return (low(grad),)
low.defvjp(low_keep, low_pass)
low_back.defvjp(back_keep, back_low)
EPSILON = 1e-06
MASKED = -1e+30

def layer_norm(values, gain, bias):
    center = values - lax.optimization_barrier(jnp.mean(values, axis=-1, keepdims=True))
    scaled = center * lax.rsqrt(lax.optimization_barrier(jnp.mean(center * center, axis=-1, keepdims=True)) + EPSILON)
    return scaled * gain + bias

def attend(block_parts):
    queries, key_rows, value_rows, keep_rows = block_parts
    scores = jnp.einsum('iphe,iqhe->ihpq', queries, key_rows, precision=lax.Precision.HIGHEST) * HEAD_DIM ** (-0.5)
    scores = low_back(scores)
    scores = jnp.where(keep_rows[:, None, None, :] > 0, scores, MASKED)
    soft_weights = low(jax.nn.softmax(scores, axis=-1))
    return jnp.einsum('ihpq,iqhe->iphe', soft_weights, value_rows, precision=lax.Precision.HIGHEST)

def forward(inputs, w_qkv, w_out, w_fc1, w_fc2, w_map, norm_gains, norm_biases, keep_float):
    highest = lax.Precision.HIGHEST
    group_size = max((size_try for size_try in range(1, 17) if IMAGES % size_try == 0))
    blocks_count = IMAGES // group_size
    normed_one = low(layer_norm(inputs, norm_gains[0], norm_biases[0]))
    project = low(low_back(jnp.einsum('rd,djc->rjc', normed_one, w_qkv, precision=highest)))
    project = project.reshape(blocks_count, group_size, PATCHES, 3, HEADS, HEAD_DIM)
    keep_blocks = keep_float.reshape(blocks_count, group_size, PATCHES)
    attended = lax.map(jax.checkpoint(attend), (project[:, :, :, 0], project[:, :, :, 1], project[:, :, :, 2], keep_blocks))
    attended = low(low_back(attended.reshape(TOKENS, D)))
    branch = low_back(jnp.einsum('rc,dc->rd', attended, w_out, precision=highest))
    middle = inputs + branch
    normed_two = low(layer_norm(middle, norm_gains[1], norm_biases[1]))
    hidden = low_back(jnp.einsum('rd,dm->rm', normed_two, w_fc1, precision=highest))
    active = low(jax.nn.gelu(hidden, approximate=False))
    outputs = middle + low_back(jnp.einsum('rm,dm->rd', active, w_fc2, precision=highest))
    normed_three = low(layer_norm(outputs, norm_gains[2], norm_biases[2]))
    logits = low_back(jnp.einsum('rd,dk->rk', normed_three, w_map, precision=highest))
    map_weights = low(jax.nn.sigmoid(logits)).reshape(IMAGES, PATCHES, MAPS) * keep_float[:, :, None]
    counts = lax.optimization_barrier(jnp.sum(keep_float, axis=1))
    pooled = jnp.einsum('ipk,ipd->ikd', map_weights, normed_three.reshape(IMAGES, PATCHES, D), precision=highest)
    return pooled * lax.rsqrt(counts)[:, None, None]

def reference(inputs, w_qkv, w_out, w_fc1, w_fc2, w_map, norm_gains, norm_biases, keep_mask, d_tokens):
    keep_float = keep_mask.astype(jnp.float32)
    primals = (inputs.astype(jnp.float32), w_qkv.astype(jnp.float32), w_out.astype(jnp.float32), w_fc1.astype(jnp.float32), w_fc2.astype(jnp.float32), w_map.astype(jnp.float32), norm_gains.astype(jnp.float32), norm_biases.astype(jnp.float32))

    def wrapped(*params):
        return forward(*params, keep_float)
    learned, pullback = jax.vjp(wrapped, *primals)
    gradients = pullback(d_tokens.astype(jnp.float32))
    return (learned, gradients[0], gradients[1], gradients[2], gradients[3], gradients[4], gradients[5], gradients[6], gradients[7])
```

```python
import jax
import jax.numpy as jnp
from jax import lax
from jax.experimental import pallas as pl
from jax.experimental.pallas import tpu as pltpu
from jax.sharding import PartitionSpec as P

HEAD_DIM = 64
EPSILON = 1e-06
MASKED = -1e30
MESH = pl.DeviceIdType.MESH

ORDERS = ("xyz", "yzx", "zxy")
SPLIT_FC1 = ((0, 384), (384, 384), (768, 256))
SPLIT_FC2 = ((0, 384), (384, 256), (640, 384))
SPLIT_OUT = (None, (0, 128), (128, 128))


def place():
    dp, t = lax.axis_index("dp"), lax.axis_index("tensor")
    return {
        "x": lax.rem(dp, 2) * 2 + t // 2,
        "y": dp // 8,
        "z": lax.rem(dp // 2, 4),
        "c": lax.rem(t, 2),
    }


def device_at(at):
    return {
        "dp": (at["y"] * 4 + at["z"]) * 2 + at["x"] // 2,
        "tensor": lax.rem(at["x"], 2) * 2 + at["c"],
    }


def moved(at, axis, by):
    return {**at, axis: lax.rem(at[axis] + by + 4, 4)}


def sibling(at):
    return {**at, "c": 1 - at["c"]}


def block(at, known):
    every = slice(None)
    xl = lax.rem(at["x"], 2) if "x" in known else every
    xh = at["x"] // 2 if "x" in known else every
    y = at["y"] if "y" in known else every
    z = at["z"] if "z" in known else every
    return (xl, at["c"], y, z, xh)


def greet(at, others):
    barrier = pltpu.get_barrier_semaphore()
    for other in others:
        pl.semaphore_signal(barrier, inc=1, device_id=device_at(other), device_id_type=MESH)
    pl.semaphore_wait(barrier, len(others))


def remote(src, dst, sends, recvs, n, target):
    return pltpu.make_async_remote_copy(
        src_ref=src,
        dst_ref=dst,
        send_sem=sends.at[n],
        recv_sem=recvs.at[n],
        device_id=device_at(target),
        device_id_type=MESH,
    )


ROWS = 208
BOTH = 2 * ROWS
CHUNK = 208
LOW = jnp.bfloat16
WIDE = jnp.float32


def dot(a, b, over=((1,), (0,))):
    return lax.dot_general(a, b, (over, ((), ())), preferred_element_type=WIDE)


NT = ((1,), (1,))
TN = ((0,), (0,))


def norm_parts(values):
    center = values - jnp.mean(values, axis=-1, keepdims=True)
    inverse = lax.rsqrt(jnp.mean(center * center, axis=-1, keepdims=True) + EPSILON)
    return center * inverse, inverse


def norm_pull(upstream, normal, inverse, gain):
    scaled = upstream * gain
    mean_grad = jnp.mean(scaled, axis=-1, keepdims=True)
    second = jnp.mean(scaled * normal, axis=-1, keepdims=True)
    return inverse * (scaled - mean_grad - normal * second)


def folded(rows):
    return jnp.sum(rows.reshape(rows.shape[0] // 8, 8, rows.shape[1]), axis=0)


def over_rows(step, carry=0):
    def body(n, carry):
        return step(pl.ds(pl.multiple_of(n * CHUNK, CHUNK), CHUNK), carry)

    return lax.fori_loop(0, BOTH // CHUNK, body, carry)


class Copies:
    def __init__(self, sends, recvs):
        self.sends, self.recvs, self.count, self.open = sends, recvs, 0, []

    def start(self, src, dst, target):
        copy = remote(src, dst, self.sends, self.recvs, self.count, target)
        self.count += 1
        copy.start()
        self.open.append(copy)
        return copy

    def left(self, gone):
        for copy in gone:
            copy.wait_send()
        self.open = [copy for copy in self.open if all(copy is not one for one in gone)]

    def finish(self):
        self.left(self.open)


class Gather:
    def __init__(self, at, copies, items):
        self.at, self.copies, self.items = at, copies, items
        self.pairs, self.siblings = {}, []

    def view(self, dst, origin, known, columns, rows=None):
        part = dst.at[block(origin, known)]
        lead = (pl.ds(*rows),) if rows else (slice(None),)
        return part.at[(Ellipsis,) + lead + (pl.ds(*columns),)]

    def to_sibling(self, part):
        self.siblings.append(self.copies.start(part, part, sibling(self.at)))

    def start(self, phase):
        at, pairs = self.at, []
        for p, order in enumerate(ORDERS):
            axis, known = order[phase], order[phase:]
            for src, dst, columns in self.items[p]:
                part = self.view(dst, at, known, columns)
                source = src.at[:, pl.ds(*columns)] if phase == 0 else part
                pair = [self.copies.start(source, part, moved(at, axis, by)) for by in (1, -1)]
                pairs.append((p, axis, known, dst, columns, pair))
                if phase == 2:
                    self.to_sibling(part)
        self.pairs[phase] = pairs

    def pass_on(self, phase):
        at = self.at
        for p, axis, known, dst, columns, pair in self.pairs[phase]:
            rows = dst.shape[-2]
            for k, by in enumerate((1, -1)):
                pair[k].wait_recv()
                origin = moved(at, axis, -by)
                if rows == 32 or by == 1:
                    half = (0 if by == 1 else 16, 16)
                    part = self.view(dst, origin, known, columns, half)
                    pair.append(self.copies.start(part, part, moved(at, axis, by)))
                if phase == 2:
                    self.to_sibling(self.view(dst, origin, known, columns))

    def end(self, phase):
        for p, axis, known, dst, columns, pair in self.pairs[phase]:
            for copy in pair[2:]:
                copy.wait_recv()
            if phase == 2:
                self.to_sibling(self.view(dst, moved(self.at, axis, 2), known, columns))

    def finish(self):
        for copy in self.siblings:
            copy.wait_recv()


def forward_kernel(
    w_qkv, w_out, w_fc1, w_fc2, w_map, tok, inputs, keep_mask, gains, biases,
    f_qkv, f_out, f_fc1, f_fc2, h_project, h_soft, h_attended, h_middle, h_two, h_active, h_slope, h_x,
    learned, d_map, grad, gain_grad, bias_grad,
    g_qkv, g_out, g_fc1, g_fc2, g_map, normed, project, soft, attended, middle, active, slope, three,
    x, raw, tokens, maps, stack,
    sends, recvs, local,
):
    at = place()
    t = lax.rem(at["x"], 2) * 2 + at["c"]
    mate = {**at, "x": at["x"] + 1 - 2 * lax.rem(at["x"], 2)}
    mates = (mate, sibling(at), sibling(mate))
    get_raw = pltpu.make_async_copy(
        inputs.at[pl.ds(pl.multiple_of(t * 392, 8), 392)], raw.at[pl.ds(0, 392)], local.at[31]
    )
    get_raw.start()
    near = [moved(at, axis, by) for axis in "xyz" for by in (1, -1)]
    greet(at, near + [sibling(at), sibling(mate)])
    copies = Copies(sends, recvs)
    locals_used = [0]

    def here(src, dst):
        copy = pltpu.make_async_copy(src, dst, local.at[locals_used[0]])
        locals_used[0] += 1
        copy.start()
        return copy

    groups = (
        Gather(at, copies, [[(w_qkv.at[p], g_qkv.at[p], (0, 256))] for p in range(3)]),
        Gather(
            at,
            copies,
            [
                [(w_map, g_map, (0, 128))],
                [(w_out, g_out, SPLIT_OUT[1])],
                [(w_out, g_out, SPLIT_OUT[2])],
            ],
        ),
        Gather(at, copies, [[(w_fc1, g_fc1, SPLIT_FC1[p])] for p in range(3)]),
        Gather(at, copies, [[(w_fc2, g_fc2, SPLIT_FC2[p])] for p in range(3)]),
    )
    for group in groups:
        group.start(0)
    mine = block(at, "xyz")
    own = [here(w_qkv.at[p], g_qkv.at[p].at[mine]) for p in range(3)]
    for src, dst in ((w_out, g_out), (w_fc1, g_fc1), (w_fc2, g_fc2), (w_map, g_map)):
        own.append(here(src, dst.at[mine]))
    own_tokens = here(tok.at[t], tokens.at[t])
    token_copies = []
    for other in mates:
        ot = lax.rem(other["x"], 2) * 2 + other["c"]
        token_copies.append(copies.start(tok.at[ot], tokens.at[t], other))

    def norm_into(source, n):
        gain, bias = gains[n : n + 1, :], biases[n : n + 1, :]

        def step(rows, carry):
            normal, _ = norm_parts(source[rows, :])
            normed[rows, :] = (normal * gain + bias).astype(LOW)
            return carry

        over_rows(step)

    get_raw.wait()
    real = lax.broadcasted_iota(jnp.int32, (ROWS, 1), 0) < 196
    x[0:ROWS, :] = jnp.where(real, raw[0:ROWS, :], 0.0)
    x[ROWS:BOTH, :] = jnp.where(real, pltpu.roll(raw[192:400, :], ROWS - 4, 0), 0.0)
    image = lax.broadcasted_iota(jnp.int32, (8, ROWS), 0)
    keep_rows = [
        jnp.sum(jnp.where(image == 2 * t + i, keep_mask[...], 0.0), axis=0, keepdims=True) for i in range(2)
    ]
    for group in groups:
        group.pass_on(0)
    norm_into(x, 0)
    for copy in own:
        copy.wait()
    groups[0].end(0)
    groups[0].start(1)
    for group in groups[1:]:
        group.end(0)
    groups[0].pass_on(1)
    groups[0].end(1)
    groups[0].start(2)
    for group in groups[1:]:
        group.start(1)
    groups[0].pass_on(2)
    for group in groups[1:]:
        group.pass_on(1)
    groups[0].end(2)
    groups[1].end(1)
    groups[1].start(2)
    groups[2].end(1)
    groups[2].start(2)
    groups[3].end(1)
    groups[0].finish()
    saved = [here(g_qkv, f_qkv), here(x, h_x)]

    for j in range(3):

        def project_step(n, carry):
            columns = pl.ds(pl.multiple_of(n * 256, 256), 256)
            weight = g_qkv[j, n // 2, lax.rem(n, 2)].reshape(1024, 256)
            project[j, :, columns] = dot(normed[...], weight).astype(LOW)
            return carry

        lax.fori_loop(0, 4, project_step, 0, unroll=4)
    saved.append(here(project, h_project))
    groups[1].pass_on(2)

    lane = lax.broadcasted_iota(jnp.int32, (1, 128), 1)
    first = jnp.where(lane < 64, 1.0, 0.0).astype(LOW)
    second = jnp.where(lane < 64, 0.0, 1.0).astype(LOW)
    is_first = lane < 64

    def attend(i, start, stop):
        rows = pl.ds(i * ROWS, ROWS)
        hide = jnp.where(keep_rows[i] > 0, 0.0, MASKED)

        def step(n, carry):
            lanes = pl.ds(pl.multiple_of(n * 128, 128), 128)
            queries = project[0, rows, lanes] * jnp.asarray(HEAD_DIM**-0.5, LOW)
            both = jnp.concatenate((queries * first, queries * second), axis=0)
            scores = dot(both, project[1, rows, lanes], NT) + hide
            exps = jnp.exp(scores - jnp.max(scores, axis=-1, keepdims=True))
            weights = (exps * (1.0 / jnp.sum(exps, axis=-1, keepdims=True))).astype(LOW)
            soft[i, n] = weights
            result = dot(weights, project[2, rows, lanes])
            attended[rows, lanes] = jnp.where(is_first, result[:ROWS], result[ROWS:]).astype(LOW)
            return carry

        lax.fori_loop(start, stop, step, 0, unroll=2)

    attend(0, 0, 4)
    groups[1].end(2)
    attend(0, 4, 8)
    groups[2].pass_on(2)
    groups[3].start(2)
    saved.append(here(soft.at[0], h_soft.at[0]))
    attend(1, 0, 4)
    groups[1].finish()
    saved.append(here(g_out, f_out))
    groups[2].end(2)
    attend(1, 4, 8)
    saved.append(here(soft.at[1], h_soft.at[1]))
    saved.append(here(attended, h_attended))

    branch = x[...]
    for k in range(4):
        weight = g_out[k // 2, k % 2].reshape(1024, 256)
        branch = branch + dot(attended[:, k * 256 : (k + 1) * 256], weight, NT)
    middle[...] = branch
    saved.append(here(middle, h_middle))
    norm_into(middle, 1)
    save_two = here(normed, h_two)
    groups[2].finish()
    saved.append(here(g_fc1, f_fc1))

    def hidden_block(k):
        def step(n, carry):
            columns = pl.ds(pl.multiple_of(n * 256, 256), 256)
            weight = g_fc1[k // 2, k % 2, :, :, :, :, columns].reshape(1024, 256)
            hidden = dot(normed[...], weight)
            half = 0.5 + 0.5 * lax.erf(hidden * (0.5**0.5))
            active[k, :, columns] = (hidden * half).astype(LOW)
            bell = jnp.exp(hidden * hidden * -0.5) * 0.3989422804014327
            slope[k, :, columns] = (half + hidden * bell).astype(LOW)
            return carry

        lax.fori_loop(0, 4, step, 0, unroll=4)

    hidden_block(0)
    hidden_block(1)
    groups[3].pass_on(2)
    hidden_block(2)
    hidden_block(3)
    saved.append(here(active, h_active))
    saved.append(here(slope, h_slope))

    total = g_map[0, 0].astype(WIDE) + g_map[0, 1].astype(WIDE)
    total = (total + g_map[1, 0].astype(WIDE) + g_map[1, 1].astype(WIDE)).reshape(512, 128)
    upper = pltpu.roll(total, 64, 1)
    maps[:, 0] = jnp.where(is_first, total, 0.0).reshape(32, 16, 128)
    maps[:, 1] = jnp.where(is_first, upper, 0.0).reshape(32, 16, 128)
    map_rows = maps[...].reshape(1024, 128).T[:8]
    own_tokens.wait()
    for copy in token_copies:
        copy.wait_recv()
    pooled, scales = [], []
    for i in range(2):
        scales.append(lax.rsqrt(jnp.sum(keep_rows[i], axis=-1, keepdims=True)))
        pooled.append((tokens[0, i] + tokens[1, i] + tokens[2, i] + tokens[3, i]) * scales[i])
    pooled = jnp.concatenate(pooled, axis=0)
    high = pooled.astype(LOW).astype(WIDE)
    stack[...] = jnp.concatenate(
        (map_rows, map_rows, high, pooled - high, jnp.zeros((80, 1024), WIDE)), axis=0
    ).astype(LOW)
    groups[3].end(2)

    def down(k):
        weight = g_fc2[k // 2, k % 2].reshape(1024, 1024)
        grad[...] = (middle if k == 0 else grad)[...] + dot(active[k], weight, NT)

    groups[3].finish()
    for k in range(4):
        down(k)
    saved.append(here(g_fc2, f_fc2))
    save_two.wait()
    norm_into(grad, 2)

    row = lax.broadcasted_iota(jnp.int32, (BOTH, 128), 0)
    column = lax.broadcasted_iota(jnp.int32, (BOTH, 128), 1)
    mine_here = ((row < ROWS) & (column < 8)) | ((row >= ROWS) & (column >= 8) & (column < 16))
    keep_column = jnp.concatenate([jnp.broadcast_to(one, (128, ROWS)).T for one in keep_rows], axis=0)
    mask = jnp.where(mine_here, keep_column, 0.0)
    result = dot(normed[...], stack[...], NT)
    map_grad = pltpu.roll(result, 112, 1) + pltpu.roll(result, 96, 1)
    sigmoid = 1.0 / (1.0 + jnp.exp(-result))
    map_low = sigmoid.astype(LOW).astype(WIDE) * mask
    logit_grad = map_grad * mask * sigmoid * (1.0 - sigmoid)
    factors = (logit_grad + pltpu.roll(map_low, 16, 1) + pltpu.roll(map_low, 32, 1)).astype(LOW)
    pooled = dot(factors, normed[...], TN)
    d_map[...] = pooled[0:8] + pooled[8:16]
    learned[0] = pooled[16:24] * scales[0]
    learned[1] = pooled[24:32] * scales[1]
    gain = gains[2:3, :]

    def pull(rows, carry):
        upstream = dot(three[rows, :], stack[...])
        normal, inverse = norm_parts(grad[rows, :])
        grad[rows, :] = norm_pull(upstream, normal, inverse, gain)
        return carry[0] + folded(upstream * normal), carry[1] + folded(upstream)

    three[...] = factors
    zero = jnp.zeros((8, 1024), WIDE)
    sums = over_rows(pull, (zero, zero))
    gain_grad[...] = jnp.sum(sums[0], axis=0, keepdims=True)
    bias_grad[...] = jnp.sum(sums[1], axis=0, keepdims=True)
    for copy in saved:
        copy.wait()
    copies.finish()


def forward(w_qkv, w_out, w_fc1, w_fc2, w_map, tok, inputs, keep_mask, gains, biases):
    def whole(rows, columns, lead=()):
        return jax.ShapeDtypeStruct(lead + (2, 2, 4, 4, 2, rows, columns), LOW)

    def low(*shape):
        return jax.ShapeDtypeStruct(shape, LOW)

    def wide(*shape):
        return jax.ShapeDtypeStruct(shape, WIDE)

    anywhere = pl.BlockSpec(memory_space=pl.ANY)
    vmem = pl.BlockSpec(memory_space=pltpu.VMEM)
    return pl.pallas_call(
        forward_kernel,
        out_shape=(
            whole(32, 256, (3,)),
            whole(32, 256),
            whole(32, 1024),
            whole(32, 1024),
            low(3, BOTH, 1024),
            low(2, 8, BOTH, ROWS),
            low(BOTH, 1024),
            wide(BOTH, 1024),
            low(BOTH, 1024),
            low(4, BOTH, 1024),
            low(4, BOTH, 1024),
            wide(BOTH, 1024),
            wide(2, 8, 1024),
            wide(8, 1024),
            wide(BOTH, 1024),
            wide(1, 1024),
            wide(1, 1024),
        ),
        in_specs=[anywhere] * 7 + [vmem] * 3,
        out_specs=(anywhere,) * 12 + (vmem,) * 5,
        scratch_shapes=[
            pltpu.VMEM((3, 2, 2, 4, 4, 2, 32, 256), LOW),
            pltpu.VMEM((2, 2, 4, 4, 2, 32, 256), LOW),
            pltpu.VMEM((2, 2, 4, 4, 2, 32, 1024), LOW),
            pltpu.VMEM((2, 2, 4, 4, 2, 32, 1024), LOW),
            pltpu.VMEM((2, 2, 4, 4, 2, 16, 128), LOW),
            pltpu.VMEM((BOTH, 1024), LOW),
            pltpu.VMEM((3, BOTH, 1024), LOW),
            pltpu.VMEM((2, 8, BOTH, ROWS), LOW),
            pltpu.VMEM((BOTH, 1024), LOW),
            pltpu.VMEM((BOTH, 1024), WIDE),
            pltpu.VMEM((4, BOTH, 1024), LOW),
            pltpu.VMEM((4, BOTH, 1024), LOW),
            pltpu.VMEM((BOTH, 128), LOW),
            pltpu.VMEM((BOTH, 1024), WIDE),
            pltpu.VMEM((400, 1024), WIDE),
            pltpu.VMEM((4, 2, 8, 1024), WIDE),
            pltpu.VMEM((32, 2, 16, 128), WIDE),
            pltpu.VMEM((128, 1024), LOW),
            pltpu.SemaphoreType.DMA((240,)),
            pltpu.SemaphoreType.DMA((240,)),
            pltpu.SemaphoreType.DMA((32,)),
        ],
        compiler_params=pltpu.CompilerParams(
            collective_id=0, has_side_effects=True, vmem_limit_bytes=62 << 20
        ),
    )(w_qkv, w_out, w_fc1, w_fc2, w_map, tok, inputs, keep_mask, gains, biases)


GROUPS = (
    (0, ((0, 384), (384, 256), (640, 384))),
    (1, ((0, 384), (384, 384), (768, 256))),
    (2, (None, (768, 128), (896, 128))),
    (2, ((0, 256), (256, 256), (512, 256))),
)


def left_over(phase, order):
    known = order[2 - phase :]
    extents = ()
    if "x" not in known:
        extents += (2,)
    if "y" not in known:
        extents += (4,)
    if "z" not in known:
        extents += (4,)
    if "x" not in known:
        extents += (2,)
    return extents


def spot(array, origin, known):
    every = slice(None)
    xl = lax.rem(origin["x"], 2) if "x" in known else every
    xh = origin["x"] // 2 if "x" in known else every
    y = origin["y"] if "y" in known else every
    z = origin["z"] if "z" in known else every
    return array.at[xl, y, z, xh]


class Reduce:
    def __init__(self, at, copies, held, split, slots, share):
        self.at, self.copies, self.held, self.split = at, copies, held, split
        self.slots, self.share, self.sent = slots, share, {}

    def send(self, phase):
        at, sent = self.at, []
        for p, order in enumerate(ORDERS):
            if self.split[p] is None:
                continue
            axis, known = order[2 - phase], order[2 - phase :]
            for by in (1, 3, 2):
                to = moved(at, axis, by)
                part = spot(self.held, to, known).at[..., pl.ds(*self.split[p])]
                sent.append(self.copies.start(part, self.slots[phase][p].at[by - 1], to))
        self.sent[phase] = sent

    def add(self, phase):
        for copy in self.sent[phase]:
            copy.wait_recv()
        for p, order in enumerate(ORDERS):
            if self.split[p] is None:
                continue
            got = self.slots[phase][p]
            mine = spot(self.held, self.at, order[2 - phase :])
            columns = pl.ds(*self.split[p])
            total = mine[..., columns].astype(WIDE) + got[0].astype(WIDE)
            total = total + got[1].astype(WIDE) + got[2].astype(WIDE)
            if phase == 2:
                if len(self.share.shape) == 3:
                    self.share[p] = total
                else:
                    start, width = self.split[p]
                    self.share[:, pl.ds(start % self.share.shape[1] if width == 128 else start, width)] = total
            else:
                mine[..., columns] = total.astype(LOW)


def backward_kernel(
    f_qkv, f_out, f_fc1, f_fc2, h_project, h_soft, h_attended, h_middle, h_two, h_active, h_slope,
    h_x, h_grad, gain_three, bias_three, d_map, learned, gains, biases,
    d_fc2, d_fc1, d_out, d_qkv, small_sum, dx_all, learned_all, h_other,
    held, staged, other, weights, slabs, soft, low, turned, turned_two, grad, total, wide,
    small, s_pair, corner,
    *rest,
):
    slots_of, (sends, recvs, local, s_sends, s_recvs) = rest[:-5], rest[-5:]
    at = place()
    c = at["c"]
    t = lax.rem(at["x"], 2) * 2 + c
    mate = {**at, "x": at["x"] + 1 - 2 * lax.rem(at["x"], 2)}
    mates = (mate, sibling(at), sibling(mate))
    mt = lax.rem(mate["x"], 2) * 2 + c
    used = [0]

    def here(src, dst):
        copy = pltpu.make_async_copy(src, dst, local.at[used[0]])
        used[0] += 1
        copy.start()
        return copy

    get_two = here(h_two, low)
    get_grad = here(h_grad, grad)
    get_active = [here(h_active.at[1 - c], slabs.at[0]), here(h_active.at[3 - c], slabs.at[1])]

    def get_columns(array, k, slot):
        return [here(array.at[k, :, pl.ds(n * 256, 256)], weights.at[slot, n]) for n in range(4)]

    turn = (1 - c, 3 - c, c, 2 + c)
    get_up = get_columns(f_fc2, turn[0], 0)
    get_slope = here(h_slope.at[turn[0]], slabs.at[2])
    get_down = get_columns(f_fc1, turn[0], 1)
    get_soft = here(h_soft.at[0], soft)
    get_middle = here(h_middle, wide)

    lines = [moved(at, axis, by) for axis in "xyz" for by in (1, 2, 3)]
    greet(at, lines + [sibling(at), sibling(mate)])
    copies = Copies(sends, recvs)

    reduces, n = [], 0
    for which, split in GROUPS:
        slots = []
        for phase in range(3):
            row = []
            for p in range(3):
                if split[p] is None:
                    row.append(None)
                else:
                    row.append(slots_of[n])
                    n += 1
            slots.append(row)
        reduces.append(Reduce(at, copies, held.at[which], split, slots, (d_fc2, d_fc1, d_out, d_qkv)[len(reduces)]))
    fc2, fc1, out, qkv = reduces

    def transpose_into(source, target):
        def step(n, carry):
            columns = pl.ds(pl.multiple_of(n * 256, 256), 256)
            target[columns, :] = source[:, columns].T
            return carry

        lax.fori_loop(0, 4, step, 0, unroll=2)

    def weight_grad(left, right, which, xl, is_own, first, count, shift=0, stage=None):
        stage = staged if stage is None else stage

        def step(n, carry):
            source = pl.ds(pl.multiple_of(n * 256, 256), 256)
            columns = pl.ds(pl.multiple_of(n * 256 + shift, 128), 256)
            result = dot(left[...], right[:, source])
            if is_own:
                result = result + other[xl, :, :, :, :, columns].reshape(1024, 256).astype(WIDE)
                held[which, xl, :, :, :, :, columns] = result.astype(LOW).reshape(4, 4, 2, 32, 256)
            else:
                stage[xl, :, :, :, :, columns] = result.astype(LOW).reshape(4, 4, 2, 32, 256)
            return carry

        lax.fori_loop(first, first + count, step, 0, unroll=count)

    def hand_over(which, xl, columns, stage=None):
        part = (staged if stage is None else stage).at[xl].at[..., pl.ds(*columns)]
        return copies.start(part, h_other.at[which, xl].at[..., pl.ds(*columns)], sibling(at))

    def take_over(copy, which, xl, columns):
        copy.wait_recv()
        part = h_other.at[which, xl].at[..., pl.ds(*columns)]
        return here(part, other.at[xl].at[..., pl.ds(*columns)])

    def up(k):
        def step(n, carry):
            columns = pl.ds(pl.multiple_of(n * 256, 256), 256)
            result = dot(low[...], weights[0, n])
            result = result * slabs[2 + k % 2, :, columns].astype(WIDE)
            slabs[4 + k, :, columns] = result.astype(LOW)
            return carry

        lax.fori_loop(0, 4, step, 0, unroll=4)

    def down(k):
        result = None if k == 0 else total[...]
        for m in range(4):
            part = dot(slabs[4 + k, :, m * 256 : (m + 1) * 256], weights[1 + k % 2, m], NT)
            result = part if result is None else result + part
        total[...] = result

    def wait_all(waiting):
        for copy in waiting:
            copy.wait()

    get_two.wait()
    transpose_into(low, turned_two)
    get_grad.wait()

    def round_grad(rows, carry):
        low[rows, :] = grad[rows, :].astype(LOW)
        return carry

    over_rows(round_grad)
    transpose_into(low, turned)
    whole = (0, 1024)
    handed_two, handed_one = [], []
    for xl in range(2):
        get_active[xl].wait()
        weight_grad(turned, slabs.at[xl], 0, xl, False, 0, 4, 0, held.at[2])
        handed_two.append(hand_over(0, xl, whole, held.at[2]))
        get_active[xl] = here(h_active.at[2 * xl + c], slabs.at[xl])
    learned_copies = [copies.start(learned, learned_all.at[t], one) for one in mates]
    own_learned = here(learned, learned_all.at[t])
    for k in range(2):
        wait_all(get_up)
        get_slope.wait()
        up(k)
        get_up = get_columns(f_fc2, turn[k + 1], 0)
        get_slope = here(h_slope.at[turn[k + 1]], slabs.at[2 + (k + 1) % 2])
        weight_grad(turned_two, slabs.at[4 + k], 1, k, False, 0, 2)
        taken = take_over(handed_two[k], 0, k, whole)
        weight_grad(turned_two, slabs.at[4 + k], 1, k, False, 2, 2)
        handed_one.append(hand_over(1, k, whole))
        get_active[k].wait()
        taken.wait()
        weight_grad(turned, slabs.at[k], 0, k, True, 0, 4)
    fc2.send(0)
    for k in range(2):
        next_down = get_columns(f_fc1, turn[k + 1], 2 - k)
        wait_all(get_down)
        down(k)
        get_down = next_down
    for k in range(2, 4):
        wait_all(get_up)
        get_slope.wait()
        taken = take_over(handed_one[k - 2], 1, k - 2, whole)
        up(k)
        if k == 2:
            get_up = get_columns(f_fc2, turn[3], 0)
            get_slope = here(h_slope.at[turn[3]], slabs.at[3])
        taken.wait()
        weight_grad(turned_two, slabs.at[4 + k], 1, k - 2, True, 0, 4)
    fc1.send(0)
    get_out = [here(f_out.at[k], weights.at[0, k]) for k in range(4)]
    next_down = get_columns(f_fc1, turn[3], 2)
    wait_all(get_down)
    down(2)
    get_qkv = [[here(f_qkv.at[0, k], weights.at[1, k]) for k in range(4)]]
    wait_all(next_down)
    down(3)
    get_qkv.append([here(f_qkv.at[1, k], weights.at[2, k]) for k in range(4)])
    attended = slabs.at[5]
    get_attended = here(h_attended, attended)
    get_project = [here(h_project.at[j], slabs.at[j]) for j in range(3)]
    get_middle.wait()
    zero = jnp.zeros((8, 1024), WIDE)

    def pull_two(rows, carry):
        upstream = total[rows, :]
        normal, inverse = norm_parts(wide[rows, :])
        result = grad[rows, :] + norm_pull(upstream, normal, inverse, gains[1:2, :])
        grad[rows, :] = result
        low[rows, :] = result.astype(LOW)
        return carry[0] + folded(upstream * normal), carry[1] + folded(upstream)

    small[...] = jnp.zeros((16, 1024), WIDE)
    small[2:3, :] = gain_three[...]
    small[5:6, :] = bias_three[...]
    small[6:14, :] = d_map[...]
    sums = over_rows(pull_two, (zero, zero))
    small[1:2, :] = jnp.sum(sums[0], axis=0, keepdims=True)
    small[4:5, :] = jnp.sum(sums[1], axis=0, keepdims=True)
    get_x = here(h_x, wide)

    transpose_into(low, turned)
    copies.left(handed_two + handed_one)
    get_attended.wait()
    out_columns = (768, 256)

    def out_grad(xl, is_own):
        right = attended.at[:, pl.ds(pl.multiple_of((2 * xl + (c if is_own else 1 - c)) * 256, 256), 256)]
        weight_grad(turned, right, 2, xl, is_own, 0, 1, 768)

    handed = []
    for xl in range(2):
        out_grad(xl, False)
        handed.append(hand_over(2, xl, out_columns))
    wait_all(get_out)
    for k in range(4):
        slabs[4, :, k * 256 : (k + 1) * 256] = dot(low[...], weights[0, k]).astype(LOW)
    get_qkv.append([here(f_qkv.at[2, k], weights.at[0, k]) for k in range(4)])
    fc2.add(0)
    fc2.send(1)
    taken = [take_over(handed[xl], 2, xl, out_columns) for xl in range(2)]
    wait_all(taken)
    for xl in range(2):
        out_grad(xl, True)
    out.send(0)
    get_x.wait()

    def normal_again(rows, carry):
        normal, _ = norm_parts(wide[rows, :])
        low[rows, :] = (normal * gains[0:1, :] + biases[0:1, :]).astype(LOW)
        return carry

    over_rows(normal_again)
    transpose_into(low, turned)

    lane = lax.broadcasted_iota(jnp.int32, (1, 128), 1)
    first = jnp.where(lane < 64, 1.0, 0.0).astype(LOW)
    second = jnp.where(lane < 64, 0.0, 1.0).astype(LOW)
    is_first = lane < 64
    factor = HEAD_DIM**-0.5
    wait_all(get_project)

    def attend(i, start, stop):
        rows = pl.ds(i * ROWS, ROWS)

        def step(n, carry):
            lanes = pl.ds(pl.multiple_of(n * 128, 128), 128)
            queries = slabs[0, rows, lanes] * jnp.asarray(factor, LOW)
            keys = slabs[1, rows, lanes]
            upstream = slabs[4, rows, lanes]
            both = jnp.concatenate((upstream * first, upstream * second), axis=0)
            chosen = soft[n]
            soft_grad = dot(both, slabs[2, rows, lanes], NT)
            wide_soft = chosen.astype(WIDE)
            product = wide_soft * soft_grad
            mean = jnp.sum(product, axis=-1, keepdims=True)
            score_grad = (product - wide_soft * mean).astype(LOW)
            result = dot(score_grad, keys)
            result = jnp.where(is_first, result[:ROWS], result[ROWS:]) * factor
            slabs[5, rows, lanes] = result.astype(LOW)
            pair = jnp.concatenate((queries * first, queries * second), axis=0)
            slabs[6, rows, lanes] = dot(score_grad, pair, TN).astype(LOW)
            slabs[7, rows, lanes] = dot(chosen, both, TN).astype(LOW)
            return carry

        lax.fori_loop(start, stop, step, 0, unroll=2)

    def finish_image(i):
        rows = pl.ds(i * ROWS, ROWS)
        upstream = None
        for j, slot in enumerate((1, 2, 0)):
            for m in range(4):
                part = dot(slabs[5 + j, rows, m * 256 : (m + 1) * 256], weights[slot, m], NT)
                upstream = part if upstream is None else upstream + part
        normal, inverse = norm_parts(wide[rows, :])
        result = grad[rows, :] + norm_pull(upstream, normal, inverse, gains[0:1, :])
        if i == 0:
            corner[...] = result[192:200]
            rows = pl.ds(0, 192)
            low[rows, :] = result[:192].astype(LOW)
        else:
            rows = pl.ds(192, 208)
            result = pltpu.roll(result, 4, 0)
            edge = lax.broadcasted_iota(jnp.int32, (8, 1), 0) < 4
            result = jnp.concatenate((jnp.where(edge, corner[...], result[:8]), result[8:]), axis=0)
            low[rows, :] = result.astype(LOW)
        sent = []
        for one in (mate, sibling(at)):
            sent.append(copies.start(low.at[rows], dx_all.at[t, rows], one))
        sent.append(here(low.at[rows], dx_all.at[t, rows]))
        return sent, folded(upstream * normal), folded(upstream)

    get_soft.wait()
    attend(0, 0, 8)
    get_soft = here(h_soft.at[1], soft)
    wait_all(get_qkv[0] + get_qkv[1] + get_qkv[2])
    images = [finish_image(0)]
    fc2.add(1)
    fc2.send(2)
    get_soft.wait()
    attend(1, 0, 4)
    fc1.add(0)
    fc1.send(1)
    attend(1, 4, 8)

    def qkv_grad(j, xl, is_own):
        right = slabs.at[5 + j, :, pl.ds(pl.multiple_of((2 * xl + (c if is_own else 1 - c)) * 256, 256), 256)]
        weight_grad(turned, right, 2, xl, is_own, 0, 1, j * 256)

    handed = []
    for j in range(3):
        for xl in range(2):
            qkv_grad(j, xl, False)
            handed.append(hand_over(2, xl, (j * 256, 256)))
    images.append(finish_image(1))
    small[0:1, :] = jnp.sum(images[0][1] + images[1][1], axis=0, keepdims=True)
    small[3:4, :] = jnp.sum(images[0][2] + images[1][2], axis=0, keepdims=True)
    s_pair[pl.ds(c, 1)] = small[...][None]
    pair = remote(small, s_pair.at[c], s_sends, s_recvs, 0, sibling(at))
    pair.start()
    taken = []
    for j in range(3):
        for xl in range(2):
            taken.append(take_over(handed[2 * j + xl], 2, xl, (j * 256, 256)))
        if j:
            for xl in range(2):
                taken[2 * j - 2 + xl].wait()
                qkv_grad(j - 1, xl, True)
    for xl in range(2):
        taken[4 + xl].wait()
        qkv_grad(2, xl, True)
    qkv.send(0)
    pair.wait()
    small[...] = s_pair[0] + s_pair[1]

    def small_send(n):
        axis = "xyz"[n]
        slots = s_pair.at[pl.ds(2 + 4 * n, 4)]
        slots[pl.ds(at[axis], 1)] = small[...][None]
        sent = []
        for by in (1, 2, 3):
            copy = remote(
                small, slots.at[at[axis]], s_sends, s_recvs, 1 + 3 * n + by - 1, moved(at, axis, by)
            )
            copy.start()
            sent.append(copy)
        return sent

    def small_add(n, sent):
        slots = s_pair.at[pl.ds(2 + 4 * n, 4)]
        for copy in sent:
            copy.wait()
        return slots[0] + slots[1] + slots[2] + slots[3]

    def pass_on(i):
        images[i][0][0].wait_recv()
        rows = pl.ds(192 * i, 192 + 16 * i)
        part = dx_all.at[mt, rows]
        return copies.start(part, part, sibling(at))

    sent = small_send(0)
    out.add(0)
    out.send(1)
    fc1.add(1)
    fc1.send(2)
    fc2.add(2)
    passed = [pass_on(0)]
    small[...] = small_add(0, sent)
    sent = small_send(1)
    out.add(1)
    out.send(2)
    fc1.add(2)
    small[...] = small_add(1, sent)
    sent = small_send(2)
    out.add(2)
    qkv.add(0)
    qkv.send(1)
    small_sum[...] = small_add(2, sent)
    passed.append(pass_on(1))
    qkv.add(1)
    qkv.send(2)
    for copy in learned_copies + passed:
        copy.wait_recv()
    for image in images:
        image[0][1].wait_recv()
        image[0][2].wait()
    own_learned.wait()
    qkv.add(2)
    copies.finish()


def backward(f_qkv, f_out, f_fc1, f_fc2, project, soft, attended, middle, two, active, slope, x, grad, gain_three, bias_three, d_map, learned, gains, biases):
    anywhere = pl.BlockSpec(memory_space=pl.ANY)
    vmem = pl.BlockSpec(memory_space=pltpu.VMEM)
    half = (2, 4, 4, 2, 32, 1024)
    slots = []
    for _, split in GROUPS:
        for phase in range(3):
            for p, order in enumerate(ORDERS):
                if split[p] is not None:
                    shape = (3,) + left_over(phase, order) + (32, split[p][1])
                    slots.append(pltpu.VMEM(shape, LOW))
    return pl.pallas_call(
        backward_kernel,
        out_shape=(
            jax.ShapeDtypeStruct((32, 1024), WIDE),
            jax.ShapeDtypeStruct((32, 1024), WIDE),
            jax.ShapeDtypeStruct((32, 256), WIDE),
            jax.ShapeDtypeStruct((3, 32, 256), WIDE),
            jax.ShapeDtypeStruct((16, 1024), WIDE),
            jax.ShapeDtypeStruct((4, 400, 1024), LOW),
            jax.ShapeDtypeStruct((4, 2, 8, 1024), WIDE),
            jax.ShapeDtypeStruct((3,) + half, LOW),
        ),
        in_specs=[anywhere] * 13 + [vmem] * 3 + [anywhere, vmem, vmem],
        out_specs=(vmem,) * 5 + (anywhere,) * 3,
        scratch_shapes=[
            pltpu.VMEM((3,) + half, LOW),
            pltpu.VMEM(half, LOW),
            pltpu.VMEM(half, LOW),
            pltpu.VMEM((3, 4, 1024, 256), LOW),
            pltpu.VMEM((8, BOTH, 1024), LOW),
            pltpu.VMEM((8, BOTH, ROWS), LOW),
            pltpu.VMEM((BOTH, 1024), LOW),
            pltpu.VMEM((1024, BOTH), LOW),
            pltpu.VMEM((1024, BOTH), LOW),
            pltpu.VMEM((BOTH, 1024), WIDE),
            pltpu.VMEM((BOTH, 1024), WIDE),
            pltpu.VMEM((BOTH, 1024), WIDE),
            pltpu.VMEM((16, 1024), WIDE),
            pltpu.VMEM((14, 16, 1024), WIDE),
            pltpu.VMEM((8, 1024), WIDE),
        ]
        + slots
        + [
            pltpu.SemaphoreType.DMA((140,)),
            pltpu.SemaphoreType.DMA((140,)),
            pltpu.SemaphoreType.DMA((100,)),
            pltpu.SemaphoreType.DMA((10,)),
            pltpu.SemaphoreType.DMA((10,)),
        ],
        compiler_params=pltpu.CompilerParams(
            collective_id=1, has_side_effects=True, vmem_limit_bytes=63 << 20
        ),
    )(f_qkv, f_out, f_fc1, f_fc2, project, soft, attended, middle, two, active, slope, x, grad, gain_three, bias_three, d_map, learned, gains, biases)


def shards(inputs, w_qkv, w_out, w_fc1, w_fc2, w_map, norm_gains, norm_biases, keep_mask, d_tokens):
    low, wide = LOW, WIDE
    t, dp = lax.axis_index("tensor"), lax.axis_index("dp")
    patches, width = keep_mask.shape[1], inputs.shape[1]

    map_share = lax.dynamic_update_slice(jnp.zeros((2, 16, 64), low), w_map.reshape(2, 16, 2), (0, 0, 2 * t))
    map_share = jnp.transpose(map_share, (1, 0, 2)).reshape(16, 128)
    tok_out = lax.dynamic_update_slice(jnp.zeros((8, 8, width), wide), d_tokens, (0, 2 * t, 0))
    keep = jnp.pad(keep_mask.astype(wide), ((0, 0), (0, ROWS - patches)))
    (
        f_qkv, f_out, f_fc1, f_fc2,
        project, soft, attended, middle, normed_two, active, slope, x,
        learned, d_map, grad, gain_three, bias_three,
    ) = forward(
        jnp.transpose(w_qkv, (1, 0, 2)), w_out, w_fc1, w_fc2, map_share,
        tok_out.reshape(4, 2, 8, width), inputs, keep, norm_gains, norm_biases,
    )
    d_fc2, d_fc1, d_out, d_qkv, small_sum, dx_all, learned_all, _ = backward(
        f_qkv.reshape(3, 4, 1024, 256),
        f_out.reshape(4, 1024, 256),
        f_fc1.reshape(4, 1024, 1024),
        f_fc2.reshape(4, 1024, 1024),
        project, soft, attended, middle, normed_two, active, slope,
        x, grad, gain_three, bias_three, d_map, learned, norm_gains, norm_biases,
    )
    map_sum = lax.dynamic_slice(small_sum, (6 + 2 * t, 32 * dp), (2, 32)).T
    return (
        lax.dynamic_slice_in_dim(learned_all.reshape(8, 8, width), 2 * t, 2, 1),
        dx_all[:, : 2 * patches].reshape(8 * patches, width).astype(wide),
        jnp.transpose(d_qkv, (1, 0, 2)),
        d_out,
        d_fc1,
        d_fc2,
        map_sum,
        small_sum[0:3],
        small_sum[3:6],
    )


def solution(mesh):
    placed = (
        P("dp", None),
        P("dp", None, "tensor"),
        P("dp", "tensor"),
        P("dp", "tensor"),
        P("dp", "tensor"),
        P("dp", "tensor"),
        P(),
        P(),
        P("dp", None),
        P("dp", "tensor", None),
    )
    return jax.shard_map(
        shards,
        mesh=mesh,
        in_specs=placed,
        out_specs=(
            P("dp", "tensor", None),
            P("dp", None),
            P("dp", None, "tensor"),
            P("dp", "tensor"),
            P("dp", "tensor"),
            P("dp", "tensor"),
            P("dp", "tensor"),
            P(),
            P(),
        ),
        check_vma=False,
    )
```

```python
import jax
import jax.numpy as jnp
from jax import lax
from jax.experimental import pallas as pl
from jax.experimental.pallas import tpu as pltpu
from jax.sharding import PartitionSpec as P

HEAD_DIM = 64
EPSILON = 1e-06
MASKED = -1e30
MESH = pl.DeviceIdType.MESH

ORDERS = ("xyz", "yzx", "zxy")
SPLIT_FC1 = ((0, 384), (384, 384), (768, 256))
SPLIT_FC2 = ((0, 384), (384, 256), (640, 384))
SPLIT_OUT = (None, (0, 128), (128, 128))


def place():
    dp, t = lax.axis_index("dp"), lax.axis_index("tensor")
    return {
        "x": lax.rem(dp, 2) * 2 + t // 2,
        "y": dp // 8,
        "z": lax.rem(dp // 2, 4),
        "c": lax.rem(t, 2),
    }


def device_at(at):
    return {
        "dp": (at["y"] * 4 + at["z"]) * 2 + at["x"] // 2,
        "tensor": lax.rem(at["x"], 2) * 2 + at["c"],
    }


def moved(at, axis, by):
    return {**at, axis: lax.rem(at[axis] + by + 4, 4)}


def sibling(at):
    return {**at, "c": 1 - at["c"]}


def block(at, known):
    every = slice(None)
    xl = lax.rem(at["x"], 2) if "x" in known else every
    xh = at["x"] // 2 if "x" in known else every
    y = at["y"] if "y" in known else every
    z = at["z"] if "z" in known else every
    return (xl, at["c"], y, z, xh)


def greet(at, others):
    barrier = pltpu.get_barrier_semaphore()
    for other in others:
        pl.semaphore_signal(barrier, inc=1, device_id=device_at(other), device_id_type=MESH)
    pl.semaphore_wait(barrier, len(others))


def remote(src, dst, sends, recvs, n, target):
    return pltpu.make_async_remote_copy(
        src_ref=src,
        dst_ref=dst,
        send_sem=sends.at[n],
        recv_sem=recvs.at[n],
        device_id=device_at(target),
        device_id_type=MESH,
    )


ROWS = 208
BOTH = 2 * ROWS
CHUNK = 208
LOW = jnp.bfloat16
WIDE = jnp.float32


def dot(a, b, over=((1,), (0,))):
    return lax.dot_general(a, b, (over, ((), ())), preferred_element_type=WIDE)


NT = ((1,), (1,))
TN = ((0,), (0,))


def norm_parts(values):
    center = values - jnp.mean(values, axis=-1, keepdims=True)
    inverse = lax.rsqrt(jnp.mean(center * center, axis=-1, keepdims=True) + EPSILON)
    return center * inverse, inverse


def norm_pull(upstream, normal, inverse, gain):
    scaled = upstream * gain
    mean_grad = jnp.mean(scaled, axis=-1, keepdims=True)
    second = jnp.mean(scaled * normal, axis=-1, keepdims=True)
    return inverse * (scaled - mean_grad - normal * second)


def folded(rows):
    return jnp.sum(rows.reshape(rows.shape[0] // 8, 8, rows.shape[1]), axis=0)


def over_rows(step, carry=0):
    def body(n, carry):
        return step(pl.ds(pl.multiple_of(n * CHUNK, CHUNK), CHUNK), carry)

    return lax.fori_loop(0, BOTH // CHUNK, body, carry)


class Copies:
    def __init__(self, sends, recvs):
        self.sends, self.recvs, self.count, self.open = sends, recvs, 0, []

    def start(self, src, dst, target):
        copy = remote(src, dst, self.sends, self.recvs, self.count, target)
        self.count += 1
        copy.start()
        self.open.append(copy)
        return copy

    def left(self, gone):
        for copy in gone:
            copy.wait_send()
        self.open = [copy for copy in self.open if all(copy is not one for one in gone)]

    def finish(self):
        self.left(self.open)


class Gather:
    def __init__(self, at, copies, items):
        self.at, self.copies, self.items = at, copies, items
        self.pairs, self.siblings = {}, []

    def view(self, dst, origin, known, columns, rows=None):
        part = dst.at[block(origin, known)]
        lead = (pl.ds(*rows),) if rows else (slice(None),)
        return part.at[(Ellipsis,) + lead + (pl.ds(*columns),)]

    def to_sibling(self, part):
        self.siblings.append(self.copies.start(part, part, sibling(self.at)))

    def start(self, phase):
        at, pairs = self.at, []
        for p, order in enumerate(ORDERS):
            axis, known = order[phase], order[phase:]
            for src, dst, columns in self.items[p]:
                part = self.view(dst, at, known, columns)
                source = src.at[:, pl.ds(*columns)] if phase == 0 else part
                pair = [self.copies.start(source, part, moved(at, axis, by)) for by in (1, -1)]
                pairs.append((p, axis, known, dst, columns, pair))
                if phase == 2:
                    self.to_sibling(part)
        self.pairs[phase] = pairs

    def pass_on(self, phase):
        at = self.at
        for p, axis, known, dst, columns, pair in self.pairs[phase]:
            rows = dst.shape[-2]
            for k, by in enumerate((1, -1)):
                pair[k].wait_recv()
                origin = moved(at, axis, -by)
                if rows == 32 or by == 1:
                    half = (0 if by == 1 else 16, 16)
                    part = self.view(dst, origin, known, columns, half)
                    pair.append(self.copies.start(part, part, moved(at, axis, by)))
                if phase == 2:
                    self.to_sibling(self.view(dst, origin, known, columns))

    def end(self, phase):
        for p, axis, known, dst, columns, pair in self.pairs[phase]:
            for copy in pair[2:]:
                copy.wait_recv()
            if phase == 2:
                self.to_sibling(self.view(dst, moved(self.at, axis, 2), known, columns))

    def finish(self):
        for copy in self.siblings:
            copy.wait_recv()


def forward_kernel(
    w_qkv, w_out, w_fc1, w_fc2, w_map, tok, inputs, keep_mask, gains, biases,
    f_qkv, f_out, f_fc1, f_fc2, h_project, h_soft, h_attended, h_middle, h_two, h_active, h_slope, h_x,
    learned, d_map, grad, gain_grad, bias_grad,
    g_qkv, g_out, g_fc1, g_fc2, g_map, normed, project, soft, attended, middle, active, slope, three,
    x, raw, tokens, maps, stack,
    sends, recvs, local,
):
    at = place()
    t = lax.rem(at["x"], 2) * 2 + at["c"]
    mate = {**at, "x": at["x"] + 1 - 2 * lax.rem(at["x"], 2)}
    mates = (mate, sibling(at), sibling(mate))
    get_raw = pltpu.make_async_copy(
        inputs.at[pl.ds(pl.multiple_of(t * 392, 8), 392)], raw.at[pl.ds(0, 392)], local.at[31]
    )
    get_raw.start()
    near = [moved(at, axis, by) for axis in "xyz" for by in (1, -1)]
    greet(at, near + [sibling(at), sibling(mate)])
    copies = Copies(sends, recvs)
    locals_used = [0]

    def here(src, dst):
        copy = pltpu.make_async_copy(src, dst, local.at[locals_used[0]])
        locals_used[0] += 1
        copy.start()
        return copy

    groups = (
        Gather(at, copies, [[(w_qkv.at[p], g_qkv.at[p], (0, 256))] for p in range(3)]),
        Gather(
            at,
            copies,
            [
                [(w_map, g_map, (0, 128))],
                [(w_out, g_out, SPLIT_OUT[1])],
                [(w_out, g_out, SPLIT_OUT[2])],
            ],
        ),
        Gather(at, copies, [[(w_fc1, g_fc1, SPLIT_FC1[p])] for p in range(3)]),
        Gather(at, copies, [[(w_fc2, g_fc2, SPLIT_FC2[p])] for p in range(3)]),
    )
    for group in groups:
        group.start(0)
    mine = block(at, "xyz")
    own = [here(w_qkv.at[p], g_qkv.at[p].at[mine]) for p in range(3)]
    for src, dst in ((w_out, g_out), (w_fc1, g_fc1), (w_fc2, g_fc2), (w_map, g_map)):
        own.append(here(src, dst.at[mine]))
    own_tokens = here(tok.at[t], tokens.at[t])
    token_copies = []
    for other in mates:
        ot = lax.rem(other["x"], 2) * 2 + other["c"]
        token_copies.append(copies.start(tok.at[ot], tokens.at[t], other))

    def norm_into(source, n):
        gain, bias = gains[n : n + 1, :], biases[n : n + 1, :]

        def step(rows, carry):
            normal, _ = norm_parts(source[rows, :])
            normed[rows, :] = (normal * gain + bias).astype(LOW)
            return carry

        over_rows(step)

    get_raw.wait()
    real = lax.broadcasted_iota(jnp.int32, (ROWS, 1), 0) < 196
    x[0:ROWS, :] = jnp.where(real, raw[0:ROWS, :], 0.0)
    x[ROWS:BOTH, :] = jnp.where(real, pltpu.roll(raw[192:400, :], ROWS - 4, 0), 0.0)
    image = lax.broadcasted_iota(jnp.int32, (8, ROWS), 0)
    keep_rows = [
        jnp.sum(jnp.where(image == 2 * t + i, keep_mask[...], 0.0), axis=0, keepdims=True) for i in range(2)
    ]
    for group in groups:
        group.pass_on(0)
    norm_into(x, 0)
    for copy in own:
        copy.wait()
    groups[0].end(0)
    groups[0].start(1)
    for group in groups[1:]:
        group.end(0)
    groups[0].pass_on(1)
    groups[0].end(1)
    groups[0].start(2)
    for group in groups[1:]:
        group.start(1)
    groups[0].pass_on(2)
    for group in groups[1:]:
        group.pass_on(1)
    groups[0].end(2)
    groups[1].end(1)
    groups[1].start(2)
    groups[2].end(1)
    groups[2].start(2)
    groups[3].end(1)
    groups[0].finish()
    saved = [here(g_qkv, f_qkv), here(x, h_x)]

    for j in range(3):

        def project_step(n, carry):
            columns = pl.ds(pl.multiple_of(n * 256, 256), 256)
            weight = g_qkv[j, n // 2, lax.rem(n, 2)].reshape(1024, 256)
            project[j, :, columns] = dot(normed[...], weight).astype(LOW)
            return carry

        lax.fori_loop(0, 4, project_step, 0, unroll=4)
    saved.append(here(project, h_project))
    groups[1].pass_on(2)

    lane = lax.broadcasted_iota(jnp.int32, (1, 128), 1)
    first = jnp.where(lane < 64, 1.0, 0.0).astype(LOW)
    second = jnp.where(lane < 64, 0.0, 1.0).astype(LOW)
    is_first = lane < 64

    def attend(i, start, stop):
        rows = pl.ds(i * ROWS, ROWS)
        hide = jnp.where(keep_rows[i] > 0, 0.0, MASKED)

        def step(n, carry):
            lanes = pl.ds(pl.multiple_of(n * 128, 128), 128)
            queries = project[0, rows, lanes] * jnp.asarray(HEAD_DIM**-0.5, LOW)
            both = jnp.concatenate((queries * first, queries * second), axis=0)
            scores = dot(both, project[1, rows, lanes], NT) + hide
            exps = jnp.exp(scores - jnp.max(scores, axis=-1, keepdims=True))
            weights = (exps * (1.0 / jnp.sum(exps, axis=-1, keepdims=True))).astype(LOW)
            soft[i, n] = weights
            result = dot(weights, project[2, rows, lanes])
            attended[rows, lanes] = jnp.where(is_first, result[:ROWS], result[ROWS:]).astype(LOW)
            return carry

        lax.fori_loop(start, stop, step, 0, unroll=2)

    attend(0, 0, 4)
    groups[1].end(2)
    attend(0, 4, 8)
    groups[2].pass_on(2)
    groups[3].start(2)
    saved.append(here(soft.at[0], h_soft.at[0]))
    attend(1, 0, 4)
    groups[1].finish()
    saved.append(here(g_out, f_out))
    groups[2].end(2)
    attend(1, 4, 8)
    saved.append(here(soft.at[1], h_soft.at[1]))
    saved.append(here(attended, h_attended))

    branch = x[...]
    for k in range(4):
        weight = g_out[k // 2, k % 2].reshape(1024, 256)
        branch = branch + dot(attended[:, k * 256 : (k + 1) * 256], weight, NT)
    middle[...] = branch
    saved.append(here(middle, h_middle))
    norm_into(middle, 1)
    save_two = here(normed, h_two)
    groups[2].finish()
    saved.append(here(g_fc1, f_fc1))

    def hidden_block(k):
        def step(n, carry):
            columns = pl.ds(pl.multiple_of(n * 256, 256), 256)
            weight = g_fc1[k // 2, k % 2, :, :, :, :, columns].reshape(1024, 256)
            hidden = dot(normed[...], weight)
            half = 0.5 + 0.5 * lax.erf(hidden * (0.5**0.5))
            active[k, :, columns] = (hidden * half).astype(LOW)
            bell = jnp.exp(hidden * hidden * -0.5) * 0.3989422804014327
            slope[k, :, columns] = (half + hidden * bell).astype(LOW)
            return carry

        lax.fori_loop(0, 4, step, 0, unroll=4)

    hidden_block(0)
    hidden_block(1)
    groups[3].pass_on(2)
    hidden_block(2)
    hidden_block(3)
    saved.append(here(active, h_active))
    saved.append(here(slope, h_slope))

    total = g_map[0, 0].astype(WIDE) + g_map[0, 1].astype(WIDE)
    total = (total + g_map[1, 0].astype(WIDE) + g_map[1, 1].astype(WIDE)).reshape(512, 128)
    upper = pltpu.roll(total, 64, 1)
    maps[:, 0] = jnp.where(is_first, total, 0.0).reshape(32, 16, 128)
    maps[:, 1] = jnp.where(is_first, upper, 0.0).reshape(32, 16, 128)
    map_rows = maps[...].reshape(1024, 128).T[:8]
    own_tokens.wait()
    for copy in token_copies:
        copy.wait_recv()
    pooled, scales = [], []
    for i in range(2):
        scales.append(lax.rsqrt(jnp.sum(keep_rows[i], axis=-1, keepdims=True)))
        pooled.append((tokens[0, i] + tokens[1, i] + tokens[2, i] + tokens[3, i]) * scales[i])
    pooled = jnp.concatenate(pooled, axis=0)
    high = pooled.astype(LOW).astype(WIDE)
    stack[...] = jnp.concatenate(
        (map_rows, map_rows, high, pooled - high, jnp.zeros((80, 1024), WIDE)), axis=0
    ).astype(LOW)
    groups[3].end(2)

    def down(k):
        weight = g_fc2[k // 2, k % 2].reshape(1024, 1024)
        grad[...] = (middle if k == 0 else grad)[...] + dot(active[k], weight, NT)

    groups[3].finish()
    for k in range(4):
        down(k)
    saved.append(here(g_fc2, f_fc2))
    save_two.wait()
    norm_into(grad, 2)

    row = lax.broadcasted_iota(jnp.int32, (BOTH, 128), 0)
    column = lax.broadcasted_iota(jnp.int32, (BOTH, 128), 1)
    mine_here = ((row < ROWS) & (column < 8)) | ((row >= ROWS) & (column >= 8) & (column < 16))
    keep_column = jnp.concatenate([jnp.broadcast_to(one, (128, ROWS)).T for one in keep_rows], axis=0)
    mask = jnp.where(mine_here, keep_column, 0.0)
    result = dot(normed[...], stack[...], NT)
    map_grad = pltpu.roll(result, 112, 1) + pltpu.roll(result, 96, 1)
    sigmoid = 1.0 / (1.0 + jnp.exp(-result))
    map_low = sigmoid.astype(LOW).astype(WIDE) * mask
    logit_grad = map_grad * mask * sigmoid * (1.0 - sigmoid)
    factors = (logit_grad + pltpu.roll(map_low, 16, 1) + pltpu.roll(map_low, 32, 1)).astype(LOW)
    pooled = dot(factors, normed[...], TN)
    d_map[...] = pooled[0:8] + pooled[8:16]
    learned[0] = pooled[16:24] * scales[0]
    learned[1] = pooled[24:32] * scales[1]
    gain = gains[2:3, :]

    def pull(rows, carry):
        upstream = dot(three[rows, :], stack[...])
        normal, inverse = norm_parts(grad[rows, :])
        grad[rows, :] = norm_pull(upstream, normal, inverse, gain)
        return carry[0] + folded(upstream * normal), carry[1] + folded(upstream)

    three[...] = factors
    zero = jnp.zeros((8, 1024), WIDE)
    sums = over_rows(pull, (zero, zero))
    gain_grad[...] = jnp.sum(sums[0], axis=0, keepdims=True)
    bias_grad[...] = jnp.sum(sums[1], axis=0, keepdims=True)
    for copy in saved:
        copy.wait()
    copies.finish()


def forward(w_qkv, w_out, w_fc1, w_fc2, w_map, tok, inputs, keep_mask, gains, biases):
    def whole(rows, columns, lead=()):
        return jax.ShapeDtypeStruct(lead + (2, 2, 4, 4, 2, rows, columns), LOW)

    def low(*shape):
        return jax.ShapeDtypeStruct(shape, LOW)

    def wide(*shape):
        return jax.ShapeDtypeStruct(shape, WIDE)

    anywhere = pl.BlockSpec(memory_space=pl.ANY)
    vmem = pl.BlockSpec(memory_space=pltpu.VMEM)
    return pl.pallas_call(
        forward_kernel,
        out_shape=(
            whole(32, 256, (3,)),
            whole(32, 256),
            whole(32, 1024),
            whole(32, 1024),
            low(3, BOTH, 1024),
            low(2, 8, BOTH, ROWS),
            low(BOTH, 1024),
            wide(BOTH, 1024),
            low(BOTH, 1024),
            low(4, BOTH, 1024),
            low(4, BOTH, 1024),
            wide(BOTH, 1024),
            wide(2, 8, 1024),
            wide(8, 1024),
            wide(BOTH, 1024),
            wide(1, 1024),
            wide(1, 1024),
        ),
        in_specs=[anywhere] * 7 + [vmem] * 3,
        out_specs=(anywhere,) * 12 + (vmem,) * 5,
        scratch_shapes=[
            pltpu.VMEM((3, 2, 2, 4, 4, 2, 32, 256), LOW),
            pltpu.VMEM((2, 2, 4, 4, 2, 32, 256), LOW),
            pltpu.VMEM((2, 2, 4, 4, 2, 32, 1024), LOW),
            pltpu.VMEM((2, 2, 4, 4, 2, 32, 1024), LOW),
            pltpu.VMEM((2, 2, 4, 4, 2, 16, 128), LOW),
            pltpu.VMEM((BOTH, 1024), LOW),
            pltpu.VMEM((3, BOTH, 1024), LOW),
            pltpu.VMEM((2, 8, BOTH, ROWS), LOW),
            pltpu.VMEM((BOTH, 1024), LOW),
            pltpu.VMEM((BOTH, 1024), WIDE),
            pltpu.VMEM((4, BOTH, 1024), LOW),
            pltpu.VMEM((4, BOTH, 1024), LOW),
            pltpu.VMEM((BOTH, 128), LOW),
            pltpu.VMEM((BOTH, 1024), WIDE),
            pltpu.VMEM((400, 1024), WIDE),
            pltpu.VMEM((4, 2, 8, 1024), WIDE),
            pltpu.VMEM((32, 2, 16, 128), WIDE),
            pltpu.VMEM((128, 1024), LOW),
            pltpu.SemaphoreType.DMA((240,)),
            pltpu.SemaphoreType.DMA((240,)),
            pltpu.SemaphoreType.DMA((32,)),
        ],
        compiler_params=pltpu.CompilerParams(
            collective_id=0, has_side_effects=True, vmem_limit_bytes=62 << 20
        ),
    )(w_qkv, w_out, w_fc1, w_fc2, w_map, tok, inputs, keep_mask, gains, biases)


GROUPS = (
    (0, ((0, 384), (384, 256), (640, 384))),
    (1, ((0, 384), (384, 256), (640, 384))),
    (2, ((768, 128), None, (896, 128))),
    (2, ((0, 384), None, (384, 384))),
)


def left_over(phase, order):
    known = order[2 - phase :]
    extents = ()
    if "x" not in known:
        extents += (2,)
    if "y" not in known:
        extents += (4,)
    if "z" not in known:
        extents += (4,)
    if "x" not in known:
        extents += (2,)
    return extents


def spot(array, origin, known):
    every = slice(None)
    xl = lax.rem(origin["x"], 2) if "x" in known else every
    xh = origin["x"] // 2 if "x" in known else every
    y = origin["y"] if "y" in known else every
    z = origin["z"] if "z" in known else every
    return array.at[xl, y, z, xh]


class Reduce:
    def __init__(self, at, copies, held, split, slots, share):
        self.at, self.copies, self.held, self.split = at, copies, held, split
        self.slots, self.share, self.sent, self.halves = slots, share, {}, []

    def parts(self, phase):
        for p, order in enumerate(ORDERS):
            if self.split[p] is not None:
                yield p, order[2 - phase], order[2 - phase :], self.split[p]

    def send(self, phase):
        sent = []
        for p, axis, known, columns in self.parts(phase):
            for by in (1, 3, 2):
                to = moved(self.at, axis, by)
                part = spot(self.held, to, known).at[..., pl.ds(*columns)]
                sent.append(self.copies.start(part, self.slots[phase][p].at[by - 1], to))
        self.sent[phase] = sent

    def start(self):
        for p, axis, known, columns in self.parts(0):
            far = spot(self.held, moved(self.at, axis, 2), known)
            for by, first in ((1, 0), (-1, 16)):
                rows = (Ellipsis, pl.ds(first, 16))
                part = far.at[rows + (pl.ds(*columns),)]
                into = self.slots[0][p].at[0].at[rows + (slice(None),)]
                self.halves.append(self.copies.start(part, into, moved(self.at, axis, by)))

    def relay(self):
        sent = []
        for n, (p, axis, known, columns) in enumerate(self.parts(0)):
            got = self.slots[0][p]
            for k, (by, first) in enumerate(((1, 0), (-1, 16))):
                self.halves[2 * n + k].wait_recv()
                to = moved(self.at, axis, by)
                rows = (Ellipsis, pl.ds(first, 16))
                part = spot(self.held, to, known)
                here = rows + (pl.ds(*columns),)
                total = part[here].astype(WIDE) + got[(0,) + rows + (slice(None),)].astype(WIDE)
                part[here] = total.astype(LOW)
                sent.append(self.copies.start(part.at[..., pl.ds(*columns)], got.at[1 + k], to))
        self.sent[0] = sent

    def add(self, phase):
        for copy in self.sent[phase]:
            copy.wait_recv()
        relayed = phase == 0 and self.halves
        for p, axis, known, columns in self.parts(phase):
            got = self.slots[phase][p]
            mine = spot(self.held, self.at, known)
            columns = pl.ds(*columns)
            total = mine[..., columns].astype(WIDE) + got[1].astype(WIDE) + got[2].astype(WIDE)
            if not relayed:
                total = total + got[0].astype(WIDE)
            if phase < 2:
                mine[..., columns] = total.astype(LOW)
                continue
            start, width = self.split[p]
            for n in range(start, start + width, 128):
                piece = total[:, n - start : n - start + 128]
                if len(self.share.shape) == 3:
                    self.share[n // 256, :, n % 256 : n % 256 + 128] = piece
                else:
                    n = n % self.share.shape[1]
                    self.share[:, n : n + 128] = piece


def backward_kernel(
    f_qkv, f_out, f_fc1, f_fc2, h_project, h_soft, h_attended, h_middle, h_two, h_active, h_slope,
    h_x, h_grad, gain_three, bias_three, d_map, learned, gains, biases,
    d_fc2, d_fc1, d_out, d_qkv, small_sum, dx_all, learned_all, h_other,
    held, staged, other, weights, slabs, soft, low, turned, turned_two, grad, total, wide,
    small, s_pair, corner,
    *rest,
):
    slots_of, (sends, recvs, local, s_sends, s_recvs) = rest[:-5], rest[-5:]
    at = place()
    c = at["c"]
    t = lax.rem(at["x"], 2) * 2 + c
    mate = {**at, "x": at["x"] + 1 - 2 * lax.rem(at["x"], 2)}
    mates = (mate, sibling(at), sibling(mate))
    mt = lax.rem(mate["x"], 2) * 2 + c
    used = [0]

    def here(src, dst):
        copy = pltpu.make_async_copy(src, dst, local.at[used[0]])
        used[0] += 1
        copy.start()
        return copy

    get_two = here(h_two, low)
    get_grad = here(h_grad, grad)
    get_active = [here(h_active.at[1 - c], slabs.at[0]), here(h_active.at[3 - c], slabs.at[1])]

    def get_columns(array, k, slot):
        return [here(array.at[k, :, pl.ds(n * 256, 256)], weights.at[slot, n]) for n in range(4)]

    turn = (1 - c, 3 - c, c, 2 + c)
    get_up = get_columns(f_fc2, turn[0], 0)
    get_slope = here(h_slope.at[turn[0]], slabs.at[2])
    get_down = get_columns(f_fc1, turn[0], 1)
    get_soft = here(h_soft.at[0], soft)
    get_middle = here(h_middle, wide)

    lines = [moved(at, axis, by) for axis in "xyz" for by in (1, 2, 3)]
    others = lines + [sibling(at), sibling(mate)]
    barrier = pltpu.get_barrier_semaphore()
    for one in others:
        pl.semaphore_signal(barrier, inc=1, device_id=device_at(one), device_id_type=MESH)
    copies = Copies(sends, recvs)

    reduces, n = [], 0
    for which, split in GROUPS:
        slots = []
        for phase in range(3):
            row = []
            for p in range(3):
                if split[p] is None:
                    row.append(None)
                else:
                    row.append(slots_of[n])
                    n += 1
            slots.append(row)
        reduces.append(Reduce(at, copies, held.at[which], split, slots, (d_fc2, d_fc1, d_out, d_qkv)[len(reduces)]))
    fc2, fc1, out, qkv = reduces

    def transpose_into(source, target):
        def step(n, carry):
            columns = pl.ds(pl.multiple_of(n * 256, 256), 256)
            target[columns, :] = source[:, columns].T
            return carry

        lax.fori_loop(0, 4, step, 0, unroll=2)

    def weight_grad(left, right, which, xl, is_own, first, count, shift=0, stage=None):
        stage = staged if stage is None else stage

        def step(n, carry):
            source = pl.ds(pl.multiple_of(n * 256, 256), 256)
            columns = pl.ds(pl.multiple_of(n * 256 + shift, 128), 256)
            result = dot(left[...], right[:, source])
            if is_own:
                result = result + other[xl, :, :, :, :, columns].reshape(1024, 256).astype(WIDE)
                held[which, xl, :, :, :, :, columns] = result.astype(LOW).reshape(4, 4, 2, 32, 256)
            else:
                stage[xl, :, :, :, :, columns] = result.astype(LOW).reshape(4, 4, 2, 32, 256)
            return carry

        lax.fori_loop(first, first + count, step, 0, unroll=count)

    def hand_over(which, xl, columns, stage=None):
        part = (staged if stage is None else stage).at[xl].at[..., pl.ds(*columns)]
        return copies.start(part, h_other.at[which, xl].at[..., pl.ds(*columns)], sibling(at))

    def take_over(copy, which, xl, columns):
        copy.wait_recv()
        part = h_other.at[which, xl].at[..., pl.ds(*columns)]
        return here(part, other.at[xl].at[..., pl.ds(*columns)])

    def up(k):
        def step(n, carry):
            columns = pl.ds(pl.multiple_of(n * 256, 256), 256)
            result = dot(low[...], weights[0, n])
            result = result * slabs[2 + k % 2, :, columns].astype(WIDE)
            slabs[4 + k, :, columns] = result.astype(LOW)
            return carry

        lax.fori_loop(0, 4, step, 0, unroll=4)

    def down(k):
        result = None if k == 0 else total[...]
        for m in range(4):
            part = dot(slabs[4 + k, :, m * 256 : (m + 1) * 256], weights[1 + k % 2, m], NT)
            result = part if result is None else result + part
        total[...] = result

    def wait_all(waiting):
        for copy in waiting:
            copy.wait()

    get_two.wait()
    transpose_into(low, turned_two)
    get_grad.wait()

    def round_grad(rows, carry):
        low[rows, :] = grad[rows, :].astype(LOW)
        return carry

    over_rows(round_grad)
    transpose_into(low, turned)
    whole = (0, 1024)
    handed_two, handed_one = [], []
    for xl in range(2):
        get_active[xl].wait()
        weight_grad(turned, slabs.at[xl], 0, xl, False, 0, 4, 0, held.at[2])
        if xl == 0:
            pl.semaphore_wait(barrier, len(others))
        handed_two.append(hand_over(0, xl, whole, held.at[2]))
        get_active[xl] = here(h_active.at[2 * xl + c], slabs.at[xl])
    learned_copies = [copies.start(learned, learned_all.at[t], one) for one in mates]
    own_learned = here(learned, learned_all.at[t])
    for k in range(2):
        wait_all(get_up)
        get_slope.wait()
        up(k)
        get_up = get_columns(f_fc2, turn[k + 1], 0)
        get_slope = here(h_slope.at[turn[k + 1]], slabs.at[2 + (k + 1) % 2])
        weight_grad(turned_two, slabs.at[4 + k], 1, k, False, 0, 2)
        taken = take_over(handed_two[k], 0, k, whole)
        weight_grad(turned_two, slabs.at[4 + k], 1, k, False, 2, 2)
        handed_one.append(hand_over(1, k, whole))
        get_active[k].wait()
        taken.wait()
        weight_grad(turned, slabs.at[k], 0, k, True, 0, 4)
    fc2.start()
    for k in range(2):
        next_down = get_columns(f_fc1, turn[k + 1], 2 - k)
        wait_all(get_down)
        down(k)
        get_down = next_down
    for k in range(2, 4):
        wait_all(get_up)
        get_slope.wait()
        taken = take_over(handed_one[k - 2], 1, k - 2, whole)
        up(k)
        if k == 2:
            get_up = get_columns(f_fc2, turn[3], 0)
            get_slope = here(h_slope.at[turn[3]], slabs.at[3])
        taken.wait()
        weight_grad(turned_two, slabs.at[4 + k], 1, k - 2, True, 0, 4)
    fc1.start()
    get_out = [here(f_out.at[k], weights.at[0, k]) for k in range(4)]
    next_down = get_columns(f_fc1, turn[3], 2)
    wait_all(get_down)
    down(2)
    fc2.relay()
    get_qkv = [[here(f_qkv.at[0, k], weights.at[1, k]) for k in range(4)]]
    wait_all(next_down)
    down(3)
    get_qkv.append([here(f_qkv.at[1, k], weights.at[2, k]) for k in range(4)])
    attended = slabs.at[5]
    get_attended = here(h_attended, attended)
    get_project = [here(h_project.at[j], slabs.at[j]) for j in range(3)]
    get_middle.wait()
    zero = jnp.zeros((8, 1024), WIDE)

    def pull_two(rows, carry):
        upstream = total[rows, :]
        normal, inverse = norm_parts(wide[rows, :])
        result = grad[rows, :] + norm_pull(upstream, normal, inverse, gains[1:2, :])
        grad[rows, :] = result
        low[rows, :] = result.astype(LOW)
        return carry[0] + folded(upstream * normal), carry[1] + folded(upstream)

    small[...] = jnp.zeros((16, 1024), WIDE)
    small[2:3, :] = gain_three[...]
    small[5:6, :] = bias_three[...]
    small[6:14, :] = d_map[...]
    sums = over_rows(pull_two, (zero, zero))
    small[1:2, :] = jnp.sum(sums[0], axis=0, keepdims=True)
    small[4:5, :] = jnp.sum(sums[1], axis=0, keepdims=True)
    get_x = here(h_x, wide)

    transpose_into(low, turned)
    copies.left(handed_two + handed_one)
    get_attended.wait()
    out_columns = (768, 256)

    def out_grad(xl, is_own):
        right = attended.at[:, pl.ds(pl.multiple_of((2 * xl + (c if is_own else 1 - c)) * 256, 256), 256)]
        weight_grad(turned, right, 2, xl, is_own, 0, 1, 768)

    handed = []
    for xl in range(2):
        out_grad(xl, False)
        handed.append(hand_over(2, xl, out_columns))
    wait_all(get_out)
    for k in range(4):
        slabs[4, :, k * 256 : (k + 1) * 256] = dot(low[...], weights[0, k]).astype(LOW)
    get_qkv.append([here(f_qkv.at[2, k], weights.at[0, k]) for k in range(4)])
    taken = [take_over(handed[xl], 2, xl, out_columns) for xl in range(2)]
    wait_all(taken)
    for xl in range(2):
        out_grad(xl, True)
    out.start()
    fc1.relay()
    get_x.wait()

    def normal_again(rows, carry):
        normal, _ = norm_parts(wide[rows, :])
        low[rows, :] = (normal * gains[0:1, :] + biases[0:1, :]).astype(LOW)
        return carry

    over_rows(normal_again)
    transpose_into(low, turned)

    lane = lax.broadcasted_iota(jnp.int32, (1, 128), 1)
    first = jnp.where(lane < 64, 1.0, 0.0).astype(LOW)
    second = jnp.where(lane < 64, 0.0, 1.0).astype(LOW)
    is_first = lane < 64
    factor = HEAD_DIM**-0.5
    wait_all(get_project)

    def attend(i, start, stop):
        rows = pl.ds(i * ROWS, ROWS)

        def step(n, carry):
            lanes = pl.ds(pl.multiple_of(n * 128, 128), 128)
            queries = slabs[0, rows, lanes] * jnp.asarray(factor, LOW)
            keys = slabs[1, rows, lanes]
            upstream = slabs[4, rows, lanes]
            both = jnp.concatenate((upstream * first, upstream * second), axis=0)
            chosen = soft[n]
            soft_grad = dot(both, slabs[2, rows, lanes], NT)
            wide_soft = chosen.astype(WIDE)
            product = wide_soft * soft_grad
            mean = jnp.sum(product, axis=-1, keepdims=True)
            score_grad = (product - wide_soft * mean).astype(LOW)
            result = dot(score_grad, keys)
            result = jnp.where(is_first, result[:ROWS], result[ROWS:]) * factor
            slabs[5, rows, lanes] = result.astype(LOW)
            pair = jnp.concatenate((queries * first, queries * second), axis=0)
            slabs[6, rows, lanes] = dot(score_grad, pair, TN).astype(LOW)
            slabs[7, rows, lanes] = dot(chosen, both, TN).astype(LOW)
            return carry

        lax.fori_loop(start, stop, step, 0, unroll=2)

    def finish_image(i):
        rows = pl.ds(i * ROWS, ROWS)
        upstream = None
        for j, slot in enumerate((1, 2, 0)):
            for m in range(4):
                part = dot(slabs[5 + j, rows, m * 256 : (m + 1) * 256], weights[slot, m], NT)
                upstream = part if upstream is None else upstream + part
        normal, inverse = norm_parts(wide[rows, :])
        result = grad[rows, :] + norm_pull(upstream, normal, inverse, gains[0:1, :])
        if i == 0:
            corner[...] = result[192:200]
            rows = pl.ds(0, 192)
            low[rows, :] = result[:192].astype(LOW)
        else:
            rows = pl.ds(192, 208)
            result = pltpu.roll(result, 4, 0)
            edge = lax.broadcasted_iota(jnp.int32, (8, 1), 0) < 4
            result = jnp.concatenate((jnp.where(edge, corner[...], result[:8]), result[8:]), axis=0)
            low[rows, :] = result.astype(LOW)
        sent = []
        for one in (mate, sibling(at)):
            sent.append(copies.start(low.at[rows], dx_all.at[t, rows], one))
        sent.append(here(low.at[rows], dx_all.at[t, rows]))
        return sent, folded(upstream * normal), folded(upstream)

    get_soft.wait()
    attend(0, 0, 4)
    fc2.add(0)
    fc2.send(1)
    out.relay()
    attend(0, 4, 8)
    get_soft = here(h_soft.at[1], soft)
    wait_all(get_qkv[0] + get_qkv[1] + get_qkv[2])
    images = [finish_image(0)]
    fc1.add(0)
    fc1.send(1)
    get_soft.wait()
    attend(1, 0, 4)
    fc2.add(1)
    fc2.send(2)
    out.add(0)
    out.send(1)
    attend(1, 4, 8)

    def qkv_grad(j, xl, is_own):
        right = slabs.at[5 + j, :, pl.ds(pl.multiple_of((2 * xl + (c if is_own else 1 - c)) * 256, 256), 256)]
        weight_grad(turned, right, 2, xl, is_own, 0, 1, j * 256)

    handed = []
    for j in range(3):
        for xl in range(2):
            qkv_grad(j, xl, False)
            handed.append(hand_over(2, xl, (j * 256, 256)))
    images.append(finish_image(1))
    small[0:1, :] = jnp.sum(images[0][1] + images[1][1], axis=0, keepdims=True)
    small[3:4, :] = jnp.sum(images[0][2] + images[1][2], axis=0, keepdims=True)
    s_pair[pl.ds(c, 1)] = small[...][None]
    pair = remote(small, s_pair.at[c], s_sends, s_recvs, 0, sibling(at))
    pair.start()
    taken = []
    for j in range(3):
        for xl in range(2):
            taken.append(take_over(handed[2 * j + xl], 2, xl, (j * 256, 256)))
        if j:
            for xl in range(2):
                taken[2 * j - 2 + xl].wait()
                qkv_grad(j - 1, xl, True)
    for xl in range(2):
        taken[4 + xl].wait()
        qkv_grad(2, xl, True)
    qkv.start()
    pair.wait()
    small[...] = s_pair[0] + s_pair[1]

    def small_send(n):
        axis = "xyz"[n]
        slots = s_pair.at[pl.ds(2 + 4 * n, 4)]
        slots[pl.ds(at[axis], 1)] = small[...][None]
        sent = []
        for by in (1, 2, 3):
            copy = remote(
                small, slots.at[at[axis]], s_sends, s_recvs, 1 + 3 * n + by - 1, moved(at, axis, by)
            )
            copy.start()
            sent.append(copy)
        return sent

    def small_add(n, sent):
        slots = s_pair.at[pl.ds(2 + 4 * n, 4)]
        for copy in sent:
            copy.wait()
        return slots[0] + slots[1] + slots[2] + slots[3]

    def pass_on(i):
        images[i][0][0].wait_recv()
        rows = pl.ds(192 * i, 192 + 16 * i)
        part = dx_all.at[mt, rows]
        return copies.start(part, part, sibling(at))

    sent = small_send(0)
    fc1.add(1)
    fc1.send(2)
    out.add(1)
    out.send(2)
    fc2.add(2)
    qkv.relay()
    small[...] = small_add(0, sent)
    sent = small_send(1)
    passed = [pass_on(0)]
    fc1.add(2)
    out.add(2)
    small[...] = small_add(1, sent)
    sent = small_send(2)
    passed.append(pass_on(1))
    qkv.add(0)
    qkv.send(1)
    small_sum[...] = small_add(2, sent)
    qkv.add(1)
    qkv.send(2)
    for copy in learned_copies + passed:
        copy.wait_recv()
    for image in images:
        image[0][1].wait_recv()
        image[0][2].wait()
    own_learned.wait()
    qkv.add(2)
    copies.finish()


def backward(f_qkv, f_out, f_fc1, f_fc2, project, soft, attended, middle, two, active, slope, x, grad, gain_three, bias_three, d_map, learned, gains, biases):
    anywhere = pl.BlockSpec(memory_space=pl.ANY)
    vmem = pl.BlockSpec(memory_space=pltpu.VMEM)
    half = (2, 4, 4, 2, 32, 1024)
    slots = []
    for _, split in GROUPS:
        for phase in range(3):
            for p, order in enumerate(ORDERS):
                if split[p] is not None:
                    shape = (3,) + left_over(phase, order) + (32, split[p][1])
                    slots.append(pltpu.VMEM(shape, LOW))
    return pl.pallas_call(
        backward_kernel,
        out_shape=(
            jax.ShapeDtypeStruct((32, 1024), WIDE),
            jax.ShapeDtypeStruct((32, 1024), WIDE),
            jax.ShapeDtypeStruct((32, 256), WIDE),
            jax.ShapeDtypeStruct((3, 32, 256), WIDE),
            jax.ShapeDtypeStruct((16, 1024), WIDE),
            jax.ShapeDtypeStruct((4, 400, 1024), LOW),
            jax.ShapeDtypeStruct((4, 2, 8, 1024), WIDE),
            jax.ShapeDtypeStruct((3,) + half, LOW),
        ),
        in_specs=[anywhere] * 13 + [vmem] * 3 + [anywhere, vmem, vmem],
        out_specs=(vmem,) * 5 + (anywhere,) * 3,
        scratch_shapes=[
            pltpu.VMEM((3,) + half, LOW),
            pltpu.VMEM(half, LOW),
            pltpu.VMEM(half, LOW),
            pltpu.VMEM((3, 4, 1024, 256), LOW),
            pltpu.VMEM((8, BOTH, 1024), LOW),
            pltpu.VMEM((8, BOTH, ROWS), LOW),
            pltpu.VMEM((BOTH, 1024), LOW),
            pltpu.VMEM((1024, BOTH), LOW),
            pltpu.VMEM((1024, BOTH), LOW),
            pltpu.VMEM((BOTH, 1024), WIDE),
            pltpu.VMEM((BOTH, 1024), WIDE),
            pltpu.VMEM((BOTH, 1024), WIDE),
            pltpu.VMEM((16, 1024), WIDE),
            pltpu.VMEM((14, 16, 1024), WIDE),
            pltpu.VMEM((8, 1024), WIDE),
        ]
        + slots
        + [
            pltpu.SemaphoreType.DMA((140,)),
            pltpu.SemaphoreType.DMA((140,)),
            pltpu.SemaphoreType.DMA((100,)),
            pltpu.SemaphoreType.DMA((10,)),
            pltpu.SemaphoreType.DMA((10,)),
        ],
        compiler_params=pltpu.CompilerParams(
            collective_id=1, has_side_effects=True, vmem_limit_bytes=63 << 20
        ),
    )(f_qkv, f_out, f_fc1, f_fc2, project, soft, attended, middle, two, active, slope, x, grad, gain_three, bias_three, d_map, learned, gains, biases)


def shards(inputs, w_qkv, w_out, w_fc1, w_fc2, w_map, norm_gains, norm_biases, keep_mask, d_tokens):
    low, wide = LOW, WIDE
    t, dp = lax.axis_index("tensor"), lax.axis_index("dp")
    patches, width = keep_mask.shape[1], inputs.shape[1]

    map_share = lax.dynamic_update_slice(jnp.zeros((2, 16, 64), low), w_map.reshape(2, 16, 2), (0, 0, 2 * t))
    map_share = jnp.transpose(map_share, (1, 0, 2)).reshape(16, 128)
    tok_out = lax.dynamic_update_slice(jnp.zeros((8, 8, width), wide), d_tokens, (0, 2 * t, 0))
    keep = jnp.pad(keep_mask.astype(wide), ((0, 0), (0, ROWS - patches)))
    (
        f_qkv, f_out, f_fc1, f_fc2,
        project, soft, attended, middle, normed_two, active, slope, x,
        learned, d_map, grad, gain_three, bias_three,
    ) = forward(
        jnp.transpose(w_qkv, (1, 0, 2)), w_out, w_fc1, w_fc2, map_share,
        tok_out.reshape(4, 2, 8, width), inputs, keep, norm_gains, norm_biases,
    )
    d_fc2, d_fc1, d_out, d_qkv, small_sum, dx_all, learned_all, _ = backward(
        f_qkv.reshape(3, 4, 1024, 256),
        f_out.reshape(4, 1024, 256),
        f_fc1.reshape(4, 1024, 1024),
        f_fc2.reshape(4, 1024, 1024),
        project, soft, attended, middle, normed_two, active, slope,
        x, grad, gain_three, bias_three, d_map, learned, norm_gains, norm_biases,
    )
    map_sum = lax.dynamic_slice(small_sum, (6 + 2 * t, 32 * dp), (2, 32)).T
    return (
        lax.dynamic_slice_in_dim(learned_all.reshape(8, 8, width), 2 * t, 2, 1),
        dx_all[:, : 2 * patches].reshape(8 * patches, width).astype(wide),
        jnp.transpose(d_qkv, (1, 0, 2)),
        d_out,
        d_fc1,
        d_fc2,
        map_sum,
        small_sum[0:3],
        small_sum[3:6],
    )


def solution(mesh):
    placed = (
        P("dp", None),
        P("dp", None, "tensor"),
        P("dp", "tensor"),
        P("dp", "tensor"),
        P("dp", "tensor"),
        P("dp", "tensor"),
        P(),
        P(),
        P("dp", None),
        P("dp", "tensor", None),
    )
    return jax.shard_map(
        shards,
        mesh=mesh,
        in_specs=placed,
        out_specs=(
            P("dp", "tensor", None),
            P("dp", None),
            P("dp", None, "tensor"),
            P("dp", "tensor"),
            P("dp", "tensor"),
            P("dp", "tensor"),
            P("dp", "tensor"),
            P(),
            P(),
        ),
        check_vma=False,
    )
```

```python
import jax
import jax.numpy as jnp
from jax import lax
from jax.experimental import pallas as pl
from jax.experimental.pallas import tpu as pltpu
from jax.sharding import PartitionSpec as P

HEAD_DIM = 64
EPSILON = 1e-06
MASKED = -1e30
MESH = pl.DeviceIdType.MESH

ORDERS = ("xyz", "yzx", "zxy")
SPLIT_FC1 = ((0, 384), (384, 384), (768, 256))
SPLIT_FC2 = ((0, 384), (384, 256), (640, 384))
SPLIT_OUT = (None, (0, 128), (128, 128))


def place():
    dp, t = lax.axis_index("dp"), lax.axis_index("tensor")
    return {
        "x": lax.rem(dp, 2) * 2 + t // 2,
        "y": dp // 8,
        "z": lax.rem(dp // 2, 4),
        "c": lax.rem(t, 2),
    }


def device_at(at):
    return {
        "dp": (at["y"] * 4 + at["z"]) * 2 + at["x"] // 2,
        "tensor": lax.rem(at["x"], 2) * 2 + at["c"],
    }


def moved(at, axis, by):
    return {**at, axis: lax.rem(at[axis] + by + 4, 4)}


def sibling(at):
    return {**at, "c": 1 - at["c"]}


def block(at, known):
    every = slice(None)
    xl = lax.rem(at["x"], 2) if "x" in known else every
    xh = at["x"] // 2 if "x" in known else every
    y = at["y"] if "y" in known else every
    z = at["z"] if "z" in known else every
    return (xl, at["c"], y, z, xh)


def greet(at, others):
    barrier = pltpu.get_barrier_semaphore()
    for other in others:
        pl.semaphore_signal(barrier, inc=1, device_id=device_at(other), device_id_type=MESH)
    pl.semaphore_wait(barrier, len(others))


def remote(src, dst, sends, recvs, n, target):
    return pltpu.make_async_remote_copy(
        src_ref=src,
        dst_ref=dst,
        send_sem=sends.at[n],
        recv_sem=recvs.at[n],
        device_id=device_at(target),
        device_id_type=MESH,
    )


ROWS = 208
BOTH = 2 * ROWS
CHUNK = 208
LOW = jnp.bfloat16
WIDE = jnp.float32


def dot(a, b, over=((1,), (0,))):
    return lax.dot_general(a, b, (over, ((), ())), preferred_element_type=WIDE)


NT = ((1,), (1,))
TN = ((0,), (0,))


def norm_parts(values):
    center = values - jnp.mean(values, axis=-1, keepdims=True)
    inverse = lax.rsqrt(jnp.mean(center * center, axis=-1, keepdims=True) + EPSILON)
    return center * inverse, inverse


def norm_pull(upstream, normal, inverse, gain):
    scaled = upstream * gain
    mean_grad = jnp.mean(scaled, axis=-1, keepdims=True)
    second = jnp.mean(scaled * normal, axis=-1, keepdims=True)
    return inverse * (scaled - mean_grad - normal * second)


def folded(rows):
    return jnp.sum(rows.reshape(rows.shape[0] // 8, 8, rows.shape[1]), axis=0)


def over_rows(step, carry=0):
    def body(n, carry):
        return step(pl.ds(pl.multiple_of(n * CHUNK, CHUNK), CHUNK), carry)

    return lax.fori_loop(0, BOTH // CHUNK, body, carry)


class Copies:
    def __init__(self, sends, recvs):
        self.sends, self.recvs, self.count, self.open = sends, recvs, 0, []

    def start(self, src, dst, target):
        copy = remote(src, dst, self.sends, self.recvs, self.count, target)
        self.count += 1
        copy.start()
        self.open.append(copy)
        return copy

    def left(self, gone):
        for copy in gone:
            copy.wait_send()
        self.open = [copy for copy in self.open if all(copy is not one for one in gone)]

    def finish(self):
        self.left(self.open)


class Gather:
    def __init__(self, at, copies, items, direct=(0,)):
        self.at, self.copies, self.items, self.direct = at, copies, items, direct
        self.pairs, self.siblings = {}, []

    def view(self, dst, origin, known, columns, rows=None):
        part = dst.at[block(origin, known)]
        lead = (pl.ds(*rows),) if rows else (slice(None),)
        return part.at[(Ellipsis,) + lead + (pl.ds(*columns),)]

    def to_sibling(self, part):
        self.siblings.append(self.copies.start(part, part, sibling(self.at)))

    def start(self, phase):
        at, pairs = self.at, []
        for p, order in enumerate(ORDERS):
            axis, known = order[phase], order[phase:]
            for src, dst, columns in self.items[p]:
                part = self.view(dst, at, known, columns)
                source = src.at[:, pl.ds(*columns)] if phase == 0 else part
                pair = [self.copies.start(source, part, moved(at, axis, by)) for by in ((1, -1, 2) if phase in self.direct else (1, -1))]
                pairs.append((p, axis, known, dst, columns, pair))
                if phase == 2:
                    self.to_sibling(part)
        self.pairs[phase] = pairs

    def pass_on(self, phase):
        at = self.at
        for p, axis, known, dst, columns, pair in self.pairs[phase]:
            if phase in self.direct:
                for copy in pair:
                    copy.wait_recv()
                continue
            rows = dst.shape[-2]
            for k, by in enumerate((1, -1)):
                pair[k].wait_recv()
                origin = moved(at, axis, -by)
                if rows == 32 or by == 1:
                    half = (0 if by == 1 else 16, 16)
                    part = self.view(dst, origin, known, columns, half)
                    pair.append(self.copies.start(part, part, moved(at, axis, by)))
                if phase == 2:
                    self.to_sibling(self.view(dst, origin, known, columns))

    def end(self, phase):
        for p, axis, known, dst, columns, pair in self.pairs[phase]:
            if phase in self.direct:
                continue
            for copy in pair[2:]:
                copy.wait_recv()
            if phase == 2:
                self.to_sibling(self.view(dst, moved(self.at, axis, 2), known, columns))

    def finish(self):
        for copy in self.siblings:
            copy.wait_recv()


def forward_kernel(
    w_qkv, w_out, w_fc1, w_fc2, w_map, tok, inputs, keep_mask, gains, biases,
    f_qkv, f_out, f_fc1, f_fc2, h_project, h_soft, h_attended, h_middle, h_two, h_active, h_slope, h_x,
    learned, d_map, grad, gain_grad, bias_grad,
    g_qkv, g_out, g_fc1, g_fc2, g_map, normed, project, soft, attended, middle, active, slope, three,
    x, raw, tokens, maps, stack,
    sends, recvs, local,
):
    at = place()
    t = lax.rem(at["x"], 2) * 2 + at["c"]
    mate = {**at, "x": at["x"] + 1 - 2 * lax.rem(at["x"], 2)}
    mates = (mate, sibling(at), sibling(mate))
    get_raw = pltpu.make_async_copy(
        inputs.at[pl.ds(pl.multiple_of(t * 392, 8), 392)], raw.at[pl.ds(0, 392)], local.at[31]
    )
    get_raw.start()
    near = [moved(at, axis, by) for axis in "xyz" for by in (1, -1, 2)]
    greet(at, near + [sibling(at), sibling(mate)])
    copies = Copies(sends, recvs)
    locals_used = [0]

    def here(src, dst):
        copy = pltpu.make_async_copy(src, dst, local.at[locals_used[0]])
        locals_used[0] += 1
        copy.start()
        return copy

    groups = (
        Gather(at, copies, [[(w_qkv.at[p], g_qkv.at[p], (0, 256))] for p in range(3)], (0, 1)),
        Gather(
            at,
            copies,
            [
                [(w_map, g_map, (0, 128))],
                [(w_out, g_out, SPLIT_OUT[1])],
                [(w_out, g_out, SPLIT_OUT[2])],
            ],
        ),
        Gather(at, copies, [[(w_fc1, g_fc1, SPLIT_FC1[p])] for p in range(3)]),
        Gather(at, copies, [[(w_fc2, g_fc2, SPLIT_FC2[p])] for p in range(3)]),
    )
    for group in groups:
        group.start(0)
    mine = block(at, "xyz")
    own = [here(w_qkv.at[p], g_qkv.at[p].at[mine]) for p in range(3)]
    for src, dst in ((w_out, g_out), (w_fc1, g_fc1), (w_fc2, g_fc2), (w_map, g_map)):
        own.append(here(src, dst.at[mine]))
    own_tokens = here(tok.at[t], tokens.at[t])
    token_copies = []
    for other in mates:
        ot = lax.rem(other["x"], 2) * 2 + other["c"]
        token_copies.append(copies.start(tok.at[ot], tokens.at[t], other))

    def norm_into(source, n):
        gain, bias = gains[n : n + 1, :], biases[n : n + 1, :]

        def step(rows, carry):
            normal, _ = norm_parts(source[rows, :])
            normed[rows, :] = (normal * gain + bias).astype(LOW)
            return carry

        over_rows(step)

    get_raw.wait()
    real = lax.broadcasted_iota(jnp.int32, (ROWS, 1), 0) < 196
    x[0:ROWS, :] = jnp.where(real, raw[0:ROWS, :], 0.0)
    x[ROWS:BOTH, :] = jnp.where(real, pltpu.roll(raw[192:400, :], ROWS - 4, 0), 0.0)
    image = lax.broadcasted_iota(jnp.int32, (8, ROWS), 0)
    keep_rows = [
        jnp.sum(jnp.where(image == 2 * t + i, keep_mask[...], 0.0), axis=0, keepdims=True) for i in range(2)
    ]
    for group in groups:
        group.pass_on(0)
    norm_into(x, 0)
    for copy in own:
        copy.wait()
    groups[0].end(0)
    groups[0].start(1)
    for group in groups[1:]:
        group.end(0)
    groups[0].pass_on(1)
    groups[0].end(1)
    groups[0].start(2)
    for group in groups[1:]:
        group.start(1)
    groups[0].pass_on(2)
    for group in groups[1:]:
        group.pass_on(1)
    groups[0].end(2)
    groups[1].end(1)
    groups[1].start(2)
    groups[2].end(1)
    groups[2].start(2)
    groups[3].end(1)
    groups[0].finish()
    saved = [here(g_qkv, f_qkv), here(x, h_x)]

    for j in range(3):

        def project_step(n, carry):
            columns = pl.ds(pl.multiple_of(n * 256, 256), 256)
            weight = g_qkv[j, n // 2, lax.rem(n, 2)].reshape(1024, 256)
            project[j, :, columns] = dot(normed[...], weight).astype(LOW)
            return carry

        lax.fori_loop(0, 4, project_step, 0, unroll=4)
    saved.append(here(project, h_project))
    groups[1].pass_on(2)

    lane = lax.broadcasted_iota(jnp.int32, (1, 128), 1)
    first = jnp.where(lane < 64, 1.0, 0.0).astype(LOW)
    second = jnp.where(lane < 64, 0.0, 1.0).astype(LOW)
    is_first = lane < 64

    def attend(i, start, stop):
        rows = pl.ds(i * ROWS, ROWS)
        hide = jnp.where(keep_rows[i] > 0, 0.0, MASKED)

        def step(n, carry):
            lanes = pl.ds(pl.multiple_of(n * 128, 128), 128)
            queries = project[0, rows, lanes] * jnp.asarray(HEAD_DIM**-0.5, LOW)
            both = jnp.concatenate((queries * first, queries * second), axis=0)
            scores = dot(both, project[1, rows, lanes], NT) + hide
            exps = jnp.exp(scores - jnp.max(scores, axis=-1, keepdims=True))
            weights = (exps * (1.0 / jnp.sum(exps, axis=-1, keepdims=True))).astype(LOW)
            soft[i, n] = weights
            result = dot(weights, project[2, rows, lanes])
            attended[rows, lanes] = jnp.where(is_first, result[:ROWS], result[ROWS:]).astype(LOW)
            return carry

        lax.fori_loop(start, stop, step, 0, unroll=2)

    attend(0, 0, 4)
    groups[1].end(2)
    attend(0, 4, 8)
    groups[2].pass_on(2)
    groups[3].start(2)
    saved.append(here(soft.at[0], h_soft.at[0]))
    attend(1, 0, 4)
    groups[1].finish()
    saved.append(here(g_out, f_out))
    groups[2].end(2)
    attend(1, 4, 8)
    saved.append(here(soft.at[1], h_soft.at[1]))
    saved.append(here(attended, h_attended))

    branch = x[...]
    for k in range(4):
        weight = g_out[k // 2, k % 2].reshape(1024, 256)
        branch = branch + dot(attended[:, k * 256 : (k + 1) * 256], weight, NT)
    middle[...] = branch
    saved.append(here(middle, h_middle))
    norm_into(middle, 1)
    save_two = here(normed, h_two)
    groups[2].finish()
    saved.append(here(g_fc1, f_fc1))

    def hidden_block(k):
        def step(n, carry):
            columns = pl.ds(pl.multiple_of(n * 256, 256), 256)
            weight = g_fc1[k // 2, k % 2, :, :, :, :, columns].reshape(1024, 256)
            hidden = dot(normed[...], weight)
            half = 0.5 + 0.5 * lax.erf(hidden * (0.5**0.5))
            active[k, :, columns] = (hidden * half).astype(LOW)
            bell = jnp.exp(hidden * hidden * -0.5) * 0.3989422804014327
            slope[k, :, columns] = (half + hidden * bell).astype(LOW)
            return carry

        lax.fori_loop(0, 4, step, 0, unroll=4)

    hidden_block(0)
    hidden_block(1)
    groups[3].pass_on(2)
    hidden_block(2)
    hidden_block(3)
    saved.append(here(active, h_active))
    saved.append(here(slope, h_slope))

    total = g_map[0, 0].astype(WIDE) + g_map[0, 1].astype(WIDE)
    total = (total + g_map[1, 0].astype(WIDE) + g_map[1, 1].astype(WIDE)).reshape(512, 128)
    upper = pltpu.roll(total, 64, 1)
    maps[:, 0] = jnp.where(is_first, total, 0.0).reshape(32, 16, 128)
    maps[:, 1] = jnp.where(is_first, upper, 0.0).reshape(32, 16, 128)
    map_rows = maps[...].reshape(1024, 128).T[:8]
    own_tokens.wait()
    for copy in token_copies:
        copy.wait_recv()
    pooled, scales = [], []
    for i in range(2):
        scales.append(lax.rsqrt(jnp.sum(keep_rows[i], axis=-1, keepdims=True)))
        pooled.append((tokens[0, i] + tokens[1, i] + tokens[2, i] + tokens[3, i]) * scales[i])
    pooled = jnp.concatenate(pooled, axis=0)
    high = pooled.astype(LOW).astype(WIDE)
    stack[...] = jnp.concatenate(
        (map_rows, map_rows, high, pooled - high, jnp.zeros((80, 1024), WIDE)), axis=0
    ).astype(LOW)
    groups[3].end(2)

    def down(xl, c, source):
        weight = g_fc2[xl, c].reshape(1024, 1024)
        grad[...] = source[...] + dot(active[2 * xl + c], weight, NT)

    down(0, at["c"], middle)
    down(1, at["c"], grad)
    groups[3].finish()
    down(0, 1 - at["c"], grad)
    down(1, 1 - at["c"], grad)
    saved.append(here(g_fc2, f_fc2))
    save_two.wait()
    norm_into(grad, 2)

    row = lax.broadcasted_iota(jnp.int32, (BOTH, 128), 0)
    column = lax.broadcasted_iota(jnp.int32, (BOTH, 128), 1)
    mine_here = ((row < ROWS) & (column < 8)) | ((row >= ROWS) & (column >= 8) & (column < 16))
    keep_column = jnp.concatenate([jnp.broadcast_to(one, (128, ROWS)).T for one in keep_rows], axis=0)
    mask = jnp.where(mine_here, keep_column, 0.0)
    result = dot(normed[...], stack[...], NT)
    map_grad = pltpu.roll(result, 112, 1) + pltpu.roll(result, 96, 1)
    sigmoid = 1.0 / (1.0 + jnp.exp(-result))
    map_low = sigmoid.astype(LOW).astype(WIDE) * mask
    logit_grad = map_grad * mask * sigmoid * (1.0 - sigmoid)
    factors = (logit_grad + pltpu.roll(map_low, 16, 1) + pltpu.roll(map_low, 32, 1)).astype(LOW)
    pooled = dot(factors, normed[...], TN)
    d_map[...] = pooled[0:8] + pooled[8:16]
    learned[0] = pooled[16:24] * scales[0]
    learned[1] = pooled[24:32] * scales[1]
    gain = gains[2:3, :]

    def pull(rows, carry):
        upstream = dot(three[rows, :], stack[...])
        normal, inverse = norm_parts(grad[rows, :])
        grad[rows, :] = norm_pull(upstream, normal, inverse, gain)
        return carry[0] + folded(upstream * normal), carry[1] + folded(upstream)

    three[...] = factors
    zero = jnp.zeros((8, 1024), WIDE)
    sums = over_rows(pull, (zero, zero))
    gain_grad[...] = jnp.sum(sums[0], axis=0, keepdims=True)
    bias_grad[...] = jnp.sum(sums[1], axis=0, keepdims=True)
    for copy in saved:
        copy.wait()
    copies.finish()


def forward(w_qkv, w_out, w_fc1, w_fc2, w_map, tok, inputs, keep_mask, gains, biases):
    def whole(rows, columns, lead=()):
        return jax.ShapeDtypeStruct(lead + (2, 2, 4, 4, 2, rows, columns), LOW)

    def low(*shape):
        return jax.ShapeDtypeStruct(shape, LOW)

    def wide(*shape):
        return jax.ShapeDtypeStruct(shape, WIDE)

    anywhere = pl.BlockSpec(memory_space=pl.ANY)
    vmem = pl.BlockSpec(memory_space=pltpu.VMEM)
    return pl.pallas_call(
        forward_kernel,
        out_shape=(
            whole(32, 256, (3,)),
            whole(32, 256),
            whole(32, 1024),
            whole(32, 1024),
            low(3, BOTH, 1024),
            low(2, 8, BOTH, ROWS),
            low(BOTH, 1024),
            wide(BOTH, 1024),
            low(BOTH, 1024),
            low(4, BOTH, 1024),
            low(4, BOTH, 1024),
            wide(BOTH, 1024),
            wide(2, 8, 1024),
            wide(8, 1024),
            wide(BOTH, 1024),
            wide(1, 1024),
            wide(1, 1024),
        ),
        in_specs=[anywhere] * 7 + [vmem] * 3,
        out_specs=(anywhere,) * 12 + (vmem,) * 5,
        scratch_shapes=[
            pltpu.VMEM((3, 2, 2, 4, 4, 2, 32, 256), LOW),
            pltpu.VMEM((2, 2, 4, 4, 2, 32, 256), LOW),
            pltpu.VMEM((2, 2, 4, 4, 2, 32, 1024), LOW),
            pltpu.VMEM((2, 2, 4, 4, 2, 32, 1024), LOW),
            pltpu.VMEM((2, 2, 4, 4, 2, 16, 128), LOW),
            pltpu.VMEM((BOTH, 1024), LOW),
            pltpu.VMEM((3, BOTH, 1024), LOW),
            pltpu.VMEM((2, 8, BOTH, ROWS), LOW),
            pltpu.VMEM((BOTH, 1024), LOW),
            pltpu.VMEM((BOTH, 1024), WIDE),
            pltpu.VMEM((4, BOTH, 1024), LOW),
            pltpu.VMEM((4, BOTH, 1024), LOW),
            pltpu.VMEM((BOTH, 128), LOW),
            pltpu.VMEM((BOTH, 1024), WIDE),
            pltpu.VMEM((400, 1024), WIDE),
            pltpu.VMEM((4, 2, 8, 1024), WIDE),
            pltpu.VMEM((32, 2, 16, 128), WIDE),
            pltpu.VMEM((128, 1024), LOW),
            pltpu.SemaphoreType.DMA((240,)),
            pltpu.SemaphoreType.DMA((240,)),
            pltpu.SemaphoreType.DMA((32,)),
        ],
        compiler_params=pltpu.CompilerParams(
            collective_id=0, has_side_effects=True, vmem_limit_bytes=62 << 20
        ),
    )(w_qkv, w_out, w_fc1, w_fc2, w_map, tok, inputs, keep_mask, gains, biases)


GROUPS = (
    (0, ((0, 384), (384, 256), (640, 384))),
    (1, ((0, 384), (384, 256), (640, 384))),
    (2, ((768, 128), None, (896, 128))),
    (2, ((0, 384), None, (384, 384))),
)


def left_over(phase, order):
    known = order[2 - phase :]
    extents = ()
    if "x" not in known:
        extents += (2,)
    if "y" not in known:
        extents += (4,)
    if "z" not in known:
        extents += (4,)
    if "x" not in known:
        extents += (2,)
    return extents


def spot(array, origin, known):
    every = slice(None)
    xl = lax.rem(origin["x"], 2) if "x" in known else every
    xh = origin["x"] // 2 if "x" in known else every
    y = origin["y"] if "y" in known else every
    z = origin["z"] if "z" in known else every
    return array.at[xl, y, z, xh]


class Reduce:
    def __init__(self, at, copies, held, split, slots, share):
        self.at, self.copies, self.held, self.split = at, copies, held, split
        self.slots, self.share, self.sent, self.halves = slots, share, {}, []

    def parts(self, phase):
        for p, order in enumerate(ORDERS):
            if self.split[p] is not None:
                yield p, order[2 - phase], order[2 - phase :], self.split[p]

    def send(self, phase):
        sent = []
        for p, axis, known, columns in self.parts(phase):
            for by in (1, 3, 2):
                to = moved(self.at, axis, by)
                part = spot(self.held, to, known).at[..., pl.ds(*columns)]
                sent.append(self.copies.start(part, self.slots[phase][p].at[by - 1], to))
        self.sent[phase] = sent

    def start(self):
        for p, axis, known, columns in self.parts(0):
            far = spot(self.held, moved(self.at, axis, 2), known)
            for by, first in ((1, 0), (-1, 16)):
                rows = (Ellipsis, pl.ds(first, 16))
                part = far.at[rows + (pl.ds(*columns),)]
                into = self.slots[0][p].at[0].at[rows + (slice(None),)]
                self.halves.append(self.copies.start(part, into, moved(self.at, axis, by)))

    def relay(self):
        sent = []
        for n, (p, axis, known, columns) in enumerate(self.parts(0)):
            got = self.slots[0][p]
            for k, (by, first) in enumerate(((1, 0), (-1, 16))):
                self.halves[2 * n + k].wait_recv()
                to = moved(self.at, axis, by)
                rows = (Ellipsis, pl.ds(first, 16))
                part = spot(self.held, to, known)
                here = rows + (pl.ds(*columns),)
                total = part[here].astype(WIDE) + got[(0,) + rows + (slice(None),)].astype(WIDE)
                part[here] = total.astype(LOW)
                sent.append(self.copies.start(part.at[..., pl.ds(*columns)], got.at[1 + k], to))
        self.sent[0] = sent

    def add(self, phase):
        for copy in self.sent[phase]:
            copy.wait_recv()
        relayed = phase == 0 and self.halves
        for p, axis, known, columns in self.parts(phase):
            got = self.slots[phase][p]
            mine = spot(self.held, self.at, known)
            columns = pl.ds(*columns)
            total = mine[..., columns].astype(WIDE) + got[1].astype(WIDE) + got[2].astype(WIDE)
            if not relayed:
                total = total + got[0].astype(WIDE)
            if phase < 2:
                mine[..., columns] = total.astype(LOW)
                continue
            start, width = self.split[p]
            for n in range(start, start + width, 128):
                piece = total[:, n - start : n - start + 128]
                if len(self.share.shape) == 3:
                    self.share[n // 256, :, n % 256 : n % 256 + 128] = piece
                else:
                    n = n % self.share.shape[1]
                    self.share[:, n : n + 128] = piece


def backward_kernel(
    f_qkv, f_out, f_fc1, f_fc2, h_project, h_soft, h_attended, h_middle, h_two, h_active, h_slope,
    h_x, h_grad, gain_three, bias_three, d_map, learned, gains, biases,
    d_fc2, d_fc1, d_out, d_qkv, small_sum, dx_all, learned_all, h_other,
    held, staged, other, weights, slabs, soft, low, turned, turned_two, grad, total, wide,
    small, s_pair, corner,
    *rest,
):
    slots_of, (sends, recvs, local, s_sends, s_recvs) = rest[:-5], rest[-5:]
    at = place()
    c = at["c"]
    t = lax.rem(at["x"], 2) * 2 + c
    mate = {**at, "x": at["x"] + 1 - 2 * lax.rem(at["x"], 2)}
    mates = (mate, sibling(at), sibling(mate))
    mt = lax.rem(mate["x"], 2) * 2 + c
    used = [0]

    def here(src, dst):
        copy = pltpu.make_async_copy(src, dst, local.at[used[0]])
        used[0] += 1
        copy.start()
        return copy

    get_two = here(h_two, low)
    get_grad = here(h_grad, grad)
    get_active = [here(h_active.at[1 - c], slabs.at[0]), here(h_active.at[3 - c], slabs.at[1])]

    def get_columns(array, k, slot):
        return [here(array.at[k, :, pl.ds(n * 256, 256)], weights.at[slot, n]) for n in range(4)]

    turn = (1 - c, 3 - c, c, 2 + c)
    get_up = get_columns(f_fc2, turn[0], 0)
    get_slope = here(h_slope.at[turn[0]], slabs.at[2])
    get_down = get_columns(f_fc1, turn[0], 1)
    get_soft = here(h_soft.at[0], soft)
    get_middle = here(h_middle, wide)

    lines = [moved(at, axis, by) for axis in "xyz" for by in (1, 2, 3)]
    others = lines + [sibling(at), sibling(mate)]
    barrier = pltpu.get_barrier_semaphore()
    for one in others:
        pl.semaphore_signal(barrier, inc=1, device_id=device_at(one), device_id_type=MESH)
    copies = Copies(sends, recvs)

    reduces, n = [], 0
    for which, split in GROUPS:
        slots = []
        for phase in range(3):
            row = []
            for p in range(3):
                if split[p] is None:
                    row.append(None)
                else:
                    row.append(slots_of[n])
                    n += 1
            slots.append(row)
        reduces.append(Reduce(at, copies, held.at[which], split, slots, (d_fc2, d_fc1, d_out, d_qkv)[len(reduces)]))
    fc2, fc1, out, qkv = reduces

    def transpose_into(source, target):
        def step(n, carry):
            columns = pl.ds(pl.multiple_of(n * 256, 256), 256)
            target[columns, :] = source[:, columns].T
            return carry

        lax.fori_loop(0, 4, step, 0, unroll=2)

    def weight_grad(left, right, which, xl, is_own, first, count, shift=0, stage=None):
        stage = staged if stage is None else stage

        def step(n, carry):
            source = pl.ds(pl.multiple_of(n * 256, 256), 256)
            columns = pl.ds(pl.multiple_of(n * 256 + shift, 128), 256)
            result = dot(left[...], right[:, source])
            if is_own:
                result = result + other[xl, :, :, :, :, columns].reshape(1024, 256).astype(WIDE)
                held[which, xl, :, :, :, :, columns] = result.astype(LOW).reshape(4, 4, 2, 32, 256)
            else:
                stage[xl, :, :, :, :, columns] = result.astype(LOW).reshape(4, 4, 2, 32, 256)
            return carry

        lax.fori_loop(first, first + count, step, 0, unroll=count)

    def hand_over(which, xl, columns, stage=None):
        part = (staged if stage is None else stage).at[xl].at[..., pl.ds(*columns)]
        return copies.start(part, h_other.at[which, xl].at[..., pl.ds(*columns)], sibling(at))

    def take_over(copy, which, xl, columns):
        copy.wait_recv()
        part = h_other.at[which, xl].at[..., pl.ds(*columns)]
        return here(part, other.at[xl].at[..., pl.ds(*columns)])

    def up(k):
        def step(n, carry):
            columns = pl.ds(pl.multiple_of(n * 256, 256), 256)
            result = dot(low[...], weights[0, n])
            result = result * slabs[2 + k % 2, :, columns].astype(WIDE)
            slabs[4 + k, :, columns] = result.astype(LOW)
            return carry

        lax.fori_loop(0, 4, step, 0, unroll=4)

    def down(k):
        result = None if k == 0 else total[...]
        for m in range(4):
            part = dot(slabs[4 + k, :, m * 256 : (m + 1) * 256], weights[1 + k % 2, m], NT)
            result = part if result is None else result + part
        total[...] = result

    def wait_all(waiting):
        for copy in waiting:
            copy.wait()

    get_two.wait()
    transpose_into(low, turned_two)
    get_grad.wait()

    def round_grad(rows, carry):
        low[rows, :] = grad[rows, :].astype(LOW)
        return carry

    over_rows(round_grad)
    transpose_into(low, turned)
    whole = (0, 1024)
    handed_two, handed_one = [], []
    for xl in range(2):
        get_active[xl].wait()
        weight_grad(turned, slabs.at[xl], 0, xl, False, 0, 4, 0, held.at[2])
        if xl == 0:
            pl.semaphore_wait(barrier, len(others))
        handed_two.append(hand_over(0, xl, whole, held.at[2]))
        get_active[xl] = here(h_active.at[2 * xl + c], slabs.at[xl])
    learned_copies = [copies.start(learned, learned_all.at[t], one) for one in mates]
    own_learned = here(learned, learned_all.at[t])
    for k in range(2):
        wait_all(get_up)
        get_slope.wait()
        up(k)
        get_up = get_columns(f_fc2, turn[k + 1], 0)
        get_slope = here(h_slope.at[turn[k + 1]], slabs.at[2 + (k + 1) % 2])
        weight_grad(turned_two, slabs.at[4 + k], 1, k, False, 0, 2)
        taken = take_over(handed_two[k], 0, k, whole)
        weight_grad(turned_two, slabs.at[4 + k], 1, k, False, 2, 2)
        handed_one.append(hand_over(1, k, whole))
        get_active[k].wait()
        taken.wait()
        weight_grad(turned, slabs.at[k], 0, k, True, 0, 4)
    fc2.start()
    for k in range(2):
        next_down = get_columns(f_fc1, turn[k + 1], 2 - k)
        wait_all(get_down)
        down(k)
        get_down = next_down
    for k in range(2, 4):
        wait_all(get_up)
        get_slope.wait()
        taken = take_over(handed_one[k - 2], 1, k - 2, whole)
        up(k)
        if k == 2:
            get_up = get_columns(f_fc2, turn[3], 0)
            get_slope = here(h_slope.at[turn[3]], slabs.at[3])
        taken.wait()
        weight_grad(turned_two, slabs.at[4 + k], 1, k - 2, True, 0, 4)
    fc1.start()
    get_out = [here(f_out.at[k], weights.at[0, k]) for k in range(4)]
    next_down = get_columns(f_fc1, turn[3], 2)
    wait_all(get_down)
    down(2)
    fc2.relay()
    get_qkv = [[here(f_qkv.at[0, k], weights.at[1, k]) for k in range(4)]]
    wait_all(next_down)
    down(3)
    get_qkv.append([here(f_qkv.at[1, k], weights.at[2, k]) for k in range(4)])
    attended = slabs.at[5]
    get_attended = here(h_attended, attended)
    get_project = [here(h_project.at[j], slabs.at[j]) for j in range(3)]
    get_middle.wait()
    zero = jnp.zeros((8, 1024), WIDE)

    def pull_two(rows, carry):
        upstream = total[rows, :]
        normal, inverse = norm_parts(wide[rows, :])
        result = grad[rows, :] + norm_pull(upstream, normal, inverse, gains[1:2, :])
        grad[rows, :] = result
        low[rows, :] = result.astype(LOW)
        return carry[0] + folded(upstream * normal), carry[1] + folded(upstream)

    small[...] = jnp.zeros((16, 1024), WIDE)
    small[2:3, :] = gain_three[...]
    small[5:6, :] = bias_three[...]
    small[6:14, :] = d_map[...]
    sums = over_rows(pull_two, (zero, zero))
    small[1:2, :] = jnp.sum(sums[0], axis=0, keepdims=True)
    small[4:5, :] = jnp.sum(sums[1], axis=0, keepdims=True)
    get_x = here(h_x, wide)

    transpose_into(low, turned)
    copies.left(handed_two + handed_one)
    get_attended.wait()
    out_columns = (768, 256)

    def out_grad(xl, is_own):
        right = attended.at[:, pl.ds(pl.multiple_of((2 * xl + (c if is_own else 1 - c)) * 256, 256), 256)]
        weight_grad(turned, right, 2, xl, is_own, 0, 1, 768)

    handed = []
    for xl in range(2):
        out_grad(xl, False)
        handed.append(hand_over(2, xl, out_columns))
    wait_all(get_out)
    for k in range(4):
        slabs[4, :, k * 256 : (k + 1) * 256] = dot(low[...], weights[0, k]).astype(LOW)
    get_qkv.append([here(f_qkv.at[2, k], weights.at[0, k]) for k in range(4)])
    taken = [take_over(handed[xl], 2, xl, out_columns) for xl in range(2)]
    wait_all(taken)
    for xl in range(2):
        out_grad(xl, True)
    out.start()
    fc1.relay()
    get_x.wait()

    def normal_again(rows, carry):
        normal, _ = norm_parts(wide[rows, :])
        low[rows, :] = (normal * gains[0:1, :] + biases[0:1, :]).astype(LOW)
        return carry

    over_rows(normal_again)
    transpose_into(low, turned)

    lane = lax.broadcasted_iota(jnp.int32, (1, 128), 1)
    first = jnp.where(lane < 64, 1.0, 0.0).astype(LOW)
    second = jnp.where(lane < 64, 0.0, 1.0).astype(LOW)
    is_first = lane < 64
    factor = HEAD_DIM**-0.5
    wait_all(get_project)

    def attend(i, start, stop):
        rows = pl.ds(i * ROWS, ROWS)

        def step(n, carry):
            lanes = pl.ds(pl.multiple_of(n * 128, 128), 128)
            queries = slabs[0, rows, lanes] * jnp.asarray(factor, LOW)
            keys = slabs[1, rows, lanes]
            upstream = slabs[4, rows, lanes]
            both = jnp.concatenate((upstream * first, upstream * second), axis=0)
            chosen = soft[n]
            soft_grad = dot(both, slabs[2, rows, lanes], NT)
            wide_soft = chosen.astype(WIDE)
            product = wide_soft * soft_grad
            mean = jnp.sum(product, axis=-1, keepdims=True)
            score_grad = (product - wide_soft * mean).astype(LOW)
            result = dot(score_grad, keys)
            result = jnp.where(is_first, result[:ROWS], result[ROWS:]) * factor
            slabs[5, rows, lanes] = result.astype(LOW)
            pair = jnp.concatenate((queries * first, queries * second), axis=0)
            slabs[6, rows, lanes] = dot(score_grad, pair, TN).astype(LOW)
            slabs[7, rows, lanes] = dot(chosen, both, TN).astype(LOW)
            return carry

        lax.fori_loop(start, stop, step, 0, unroll=2)

    def finish_image(i):
        rows = pl.ds(i * ROWS, ROWS)
        upstream = None
        for j, slot in enumerate((1, 2, 0)):
            for m in range(4):
                part = dot(slabs[5 + j, rows, m * 256 : (m + 1) * 256], weights[slot, m], NT)
                upstream = part if upstream is None else upstream + part
        normal, inverse = norm_parts(wide[rows, :])
        result = grad[rows, :] + norm_pull(upstream, normal, inverse, gains[0:1, :])
        if i == 0:
            corner[...] = result[192:200]
            rows = pl.ds(0, 192)
            low[rows, :] = result[:192].astype(LOW)
        else:
            rows = pl.ds(192, 208)
            result = pltpu.roll(result, 4, 0)
            edge = lax.broadcasted_iota(jnp.int32, (8, 1), 0) < 4
            result = jnp.concatenate((jnp.where(edge, corner[...], result[:8]), result[8:]), axis=0)
            low[rows, :] = result.astype(LOW)
        sent = []
        for one in (mate, sibling(at)):
            sent.append(copies.start(low.at[rows], dx_all.at[t, rows], one))
        sent.append(here(low.at[rows], dx_all.at[t, rows]))
        return sent, folded(upstream * normal), folded(upstream)

    get_soft.wait()
    attend(0, 0, 8)
    fc2.add(0)
    fc2.send(1)
    out.relay()
    get_soft = here(h_soft.at[1], soft)
    wait_all(get_qkv[0] + get_qkv[1] + get_qkv[2])
    images = [finish_image(0)]
    get_soft.wait()
    attend(1, 0, 4)
    fc1.add(0)
    fc1.send(1)
    attend(1, 4, 8)

    def qkv_grad(j, xl, is_own):
        right = slabs.at[5 + j, :, pl.ds(pl.multiple_of((2 * xl + (c if is_own else 1 - c)) * 256, 256), 256)]
        weight_grad(turned, right, 2, xl, is_own, 0, 1, j * 256)

    handed = []
    for j in range(3):
        for xl in range(2):
            qkv_grad(j, xl, False)
            handed.append(hand_over(2, xl, (j * 256, 256)))
    images.append(finish_image(1))
    small[0:1, :] = jnp.sum(images[0][1] + images[1][1], axis=0, keepdims=True)
    small[3:4, :] = jnp.sum(images[0][2] + images[1][2], axis=0, keepdims=True)
    s_pair[pl.ds(c, 1)] = small[...][None]
    pair = remote(small, s_pair.at[c], s_sends, s_recvs, 0, sibling(at))
    pair.start()

    def small_send(n):
        axis = "zyx"[n]
        slots = s_pair.at[pl.ds(2 + 4 * n, 4)]
        slots[pl.ds(at[axis], 1)] = small[...][None]
        sent = []
        for by in (1, 2, 3):
            copy = remote(
                small, slots.at[at[axis]], s_sends, s_recvs, 1 + 3 * n + by - 1, moved(at, axis, by)
            )
            copy.start()
            sent.append(copy)
        return sent

    def small_add(n, sent):
        slots = s_pair.at[pl.ds(2 + 4 * n, 4)]
        for copy in sent:
            copy.wait()
        return slots[0] + slots[1] + slots[2] + slots[3]

    def pass_on(i):
        images[i][0][0].wait_recv()
        rows = pl.ds(192 * i, 192 + 16 * i)
        part = dx_all.at[mt, rows]
        return copies.start(part, part, sibling(at))

    def take_qkv(j):
        return [take_over(handed[2 * j + xl], 2, xl, (j * 256, 256)) for xl in range(2)]

    def own_qkv(j, taken):
        wait_all(taken)
        for xl in range(2):
            qkv_grad(j, xl, True)

    taken = [take_qkv(0)]
    pair.wait()
    small[...] = s_pair[0] + s_pair[1]
    sent = small_send(0)
    taken.append(take_qkv(1))
    own_qkv(0, taken[0])
    out.add(0)
    out.send(1)
    taken.append(take_qkv(2))
    own_qkv(1, taken[1])
    small[...] = small_add(0, sent)
    sent = small_send(1)
    own_qkv(2, taken[2])
    qkv.start()
    fc2.add(1)
    fc2.send(2)
    small[...] = small_add(1, sent)
    sent = small_send(2)
    fc1.add(1)
    fc1.send(2)
    qkv.relay()
    passed = [pass_on(0)]
    out.add(1)
    out.send(2)
    fc2.add(2)
    fc1.add(2)
    passed.append(pass_on(1))
    out.add(2)
    qkv.add(0)
    qkv.send(1)
    small_sum[...] = small_add(2, sent)
    qkv.add(1)
    qkv.send(2)
    for copy in learned_copies + passed:
        copy.wait_recv()
    for image in images:
        image[0][1].wait_recv()
        image[0][2].wait()
    own_learned.wait()
    qkv.add(2)
    copies.finish()


def backward(f_qkv, f_out, f_fc1, f_fc2, project, soft, attended, middle, two, active, slope, x, grad, gain_three, bias_three, d_map, learned, gains, biases):
    anywhere = pl.BlockSpec(memory_space=pl.ANY)
    vmem = pl.BlockSpec(memory_space=pltpu.VMEM)
    half = (2, 4, 4, 2, 32, 1024)
    slots = []
    for _, split in GROUPS:
        for phase in range(3):
            for p, order in enumerate(ORDERS):
                if split[p] is not None:
                    shape = (3,) + left_over(phase, order) + (32, split[p][1])
                    slots.append(pltpu.VMEM(shape, LOW))
    return pl.pallas_call(
        backward_kernel,
        out_shape=(
            jax.ShapeDtypeStruct((32, 1024), WIDE),
            jax.ShapeDtypeStruct((32, 1024), WIDE),
            jax.ShapeDtypeStruct((32, 256), WIDE),
            jax.ShapeDtypeStruct((3, 32, 256), WIDE),
            jax.ShapeDtypeStruct((16, 1024), WIDE),
            jax.ShapeDtypeStruct((4, 400, 1024), LOW),
            jax.ShapeDtypeStruct((4, 2, 8, 1024), WIDE),
            jax.ShapeDtypeStruct((3,) + half, LOW),
        ),
        in_specs=[anywhere] * 13 + [vmem] * 3 + [anywhere, vmem, vmem],
        out_specs=(vmem,) * 5 + (anywhere,) * 3,
        scratch_shapes=[
            pltpu.VMEM((3,) + half, LOW),
            pltpu.VMEM(half, LOW),
            pltpu.VMEM(half, LOW),
            pltpu.VMEM((3, 4, 1024, 256), LOW),
            pltpu.VMEM((8, BOTH, 1024), LOW),
            pltpu.VMEM((8, BOTH, ROWS), LOW),
            pltpu.VMEM((BOTH, 1024), LOW),
            pltpu.VMEM((1024, BOTH), LOW),
            pltpu.VMEM((1024, BOTH), LOW),
            pltpu.VMEM((BOTH, 1024), WIDE),
            pltpu.VMEM((BOTH, 1024), WIDE),
            pltpu.VMEM((BOTH, 1024), WIDE),
            pltpu.VMEM((16, 1024), WIDE),
            pltpu.VMEM((14, 16, 1024), WIDE),
            pltpu.VMEM((8, 1024), WIDE),
        ]
        + slots
        + [
            pltpu.SemaphoreType.DMA((140,)),
            pltpu.SemaphoreType.DMA((140,)),
            pltpu.SemaphoreType.DMA((100,)),
            pltpu.SemaphoreType.DMA((10,)),
            pltpu.SemaphoreType.DMA((10,)),
        ],
        compiler_params=pltpu.CompilerParams(
            collective_id=1, has_side_effects=True, vmem_limit_bytes=63 << 20
        ),
    )(f_qkv, f_out, f_fc1, f_fc2, project, soft, attended, middle, two, active, slope, x, grad, gain_three, bias_three, d_map, learned, gains, biases)


def widen_kernel(packed, result):
    result[...] = packed[0, : result.shape[0]].astype(WIDE)


def widen(packed, rows):
    blocks, extent, width = packed.shape
    return pl.pallas_call(
        widen_kernel,
        grid=(blocks,),
        out_shape=jax.ShapeDtypeStruct((blocks * rows, width), WIDE),
        in_specs=[pl.BlockSpec((1, extent, width), lambda n: (n, 0, 0))],
        out_specs=pl.BlockSpec((rows, width), lambda n: (n, 0)),
        compiler_params=pltpu.CompilerParams(vmem_limit_bytes=24 << 20),
    )(packed)


def shards(inputs, w_qkv, w_out, w_fc1, w_fc2, w_map, norm_gains, norm_biases, keep_mask, d_tokens):
    low, wide = LOW, WIDE
    t, dp = lax.axis_index("tensor"), lax.axis_index("dp")
    patches, width = keep_mask.shape[1], inputs.shape[1]

    map_share = lax.dynamic_update_slice(jnp.zeros((2, 16, 64), low), w_map.reshape(2, 16, 2), (0, 0, 2 * t))
    map_share = jnp.transpose(map_share, (1, 0, 2)).reshape(16, 128)
    tok_out = lax.dynamic_update_slice(jnp.zeros((8, 8, width), wide), d_tokens, (0, 2 * t, 0))
    keep = jnp.pad(keep_mask.astype(wide), ((0, 0), (0, ROWS - patches)))
    (
        f_qkv, f_out, f_fc1, f_fc2,
        project, soft, attended, middle, normed_two, active, slope, x,
        learned, d_map, grad, gain_three, bias_three,
    ) = forward(
        jnp.transpose(w_qkv, (1, 0, 2)), w_out, w_fc1, w_fc2, map_share,
        tok_out.reshape(4, 2, 8, width), inputs, keep, norm_gains, norm_biases,
    )
    d_fc2, d_fc1, d_out, d_qkv, small_sum, dx_all, learned_all, _ = backward(
        f_qkv.reshape(3, 4, 1024, 256),
        f_out.reshape(4, 1024, 256),
        f_fc1.reshape(4, 1024, 1024),
        f_fc2.reshape(4, 1024, 1024),
        project, soft, attended, middle, normed_two, active, slope,
        x, grad, gain_three, bias_three, d_map, learned, norm_gains, norm_biases,
    )
    map_sum = lax.dynamic_slice(small_sum, (6 + 2 * t, 32 * dp), (2, 32)).T
    return (
        lax.dynamic_slice_in_dim(learned_all.reshape(8, 8, width), 2 * t, 2, 1),
        widen(dx_all, 2 * patches),
        jnp.transpose(d_qkv, (1, 0, 2)),
        d_out,
        d_fc1,
        d_fc2,
        map_sum,
        small_sum[0:3],
        small_sum[3:6],
    )


def solution(mesh):
    placed = (
        P("dp", None),
        P("dp", None, "tensor"),
        P("dp", "tensor"),
        P("dp", "tensor"),
        P("dp", "tensor"),
        P("dp", "tensor"),
        P(),
        P(),
        P("dp", None),
        P("dp", "tensor", None),
    )
    return jax.shard_map(
        shards,
        mesh=mesh,
        in_specs=placed,
        out_specs=(
            P("dp", "tensor", None),
            P("dp", None),
            P("dp", None, "tensor"),
            P("dp", "tensor"),
            P("dp", "tensor"),
            P("dp", "tensor"),
            P("dp", "tensor"),
            P(),
            P(),
        ),
        check_vma=False,
    )
```
